32 devices in a mesh: space: 8 (over y, x, core), chaos: 4 (over z).
Axes of the slice: x: 2, y: 2, z: 4, core: 2. Of those that a mesh axis runs over, the one named last changes fastest.
Arguments:
- forcing: float32 [288, 128, 128], P('chaos', 'space'), may hold values from -12 to 12, as said below
- start_guess: float32 [288, 128, 128], P('chaos', 'space'), may hold values from -2 to 2, as said below
- mean_field: float32 [128, 128], P('space'), may hold values from 1 to 2
- mode_fields: float32 [10, 128, 128], P(None, 'space'), may hold values from -0.04 to 0.04
- multi_index: int32 [288, 10], P('chaos'), may hold values from -1 to 3, as said below
- coupled_slot: int32 [288, 20], P('chaos'), may hold values from 0 to 288, as said below
Outputs:
- approximation: float32 [288, 128, 128], P('chaos', 'space')
- recursive_residual: float32 [288, 128, 128], P('chaos', 'space')
The draws below stay inside these ranges and needn't reach their ends.
Inputs may be any that keep to these rules, and one draw needn't show every extreme that they name: `multi_index`: row s is the multi-index of the chaos term placed in slot s: 10 nonnegative entries summing to at most 3, each such multi-index in exactly one slot; the slots without a term hold -1 in every entry. `coupled_slot`: entry (s, k) for k < 10 is the slot whose multi-index is that of slot s with one more in mode k, entry (s, 10 + k) the slot with one less in mode k; 288 where no such term exists or slot s holds no term. `forcing`: zero in the slots that hold no term. `start_guess`: zero in the slots that hold no term.
All inputs are finite; a program needn't handle non-finite values.
Results may differ from the reference program's by a relative error of at most 0.0003.
Values sent between devices are 32-bit elements; how exact they have to be, the bound alone decides.
No kernel may reach another device: no remote copies, remote signals or barrier semaphores. Data moves between devices by JAX's collectives and lax.ppermute only.
A program may use at most 128 MiB of HBM per device.

```python
import math
import jax
import jax.numpy as jnp
import numpy as np

MODES = 10
DEGREE = 3
TERMS = 286
SLOTS = 288
ROWS = 128
COLUMNS = 128
ITERS = 2


def build_indices(mode_count, remaining):
    if mode_count == 0:
        return [[]]
    listed = []
    for leading in range(remaining + 1):
        for tail_part in build_indices(mode_count - 1, remaining - leading):
            listed.append([leading] + tail_part)
    return listed


def term_tables(mode_count, degree_most):
    listed = sorted(build_indices(mode_count, degree_most), key=sum)
    lookup = {}
    for position, entry in enumerate(listed):
        lookup[tuple(entry)] = position
    term_count = len(listed)
    raising = np.full((term_count, mode_count), term_count, np.int32)
    lowering = np.full((term_count, mode_count), term_count, np.int32)
    for position, entry in enumerate(listed):
        for kl_mode in range(mode_count):
            higher = list(entry)
            higher[kl_mode] = higher[kl_mode] + 1
            raising[position, kl_mode] = lookup.get(tuple(higher), term_count)
            if entry[kl_mode] > 0:
                lowered_entry = list(entry)
                lowered_entry[kl_mode] = lowered_entry[kl_mode] - 1
                lowering[position, kl_mode] = lookup[tuple(lowered_entry)]
    return (np.array(listed, np.int32), raising, lowering)


def slot_layout(key):
    term_table, raising, lowering = term_tables(MODES, DEGREE)
    holder = jax.random.permutation(jax.random.fold_in(key, 11), SLOTS).astype(jnp.int32)
    slot_of = jnp.argsort(holder, stable=True).astype(jnp.int32)
    slot_ext = jnp.concatenate([slot_of[:TERMS], jnp.full((1,), SLOTS, jnp.int32)])
    living = holder < TERMS
    clipped = jnp.minimum(holder, TERMS - 1)
    multi_rows = jnp.where(living[:, None], jnp.asarray(term_table)[clipped], -1).astype(jnp.int32)
    raised = slot_ext[jnp.asarray(raising)[clipped]]
    lowered = slot_ext[jnp.asarray(lowering)[clipped]]
    coupled = jnp.where(living[:, None], jnp.concatenate([raised, lowered], axis=1), SLOTS).astype(jnp.int32)
    return (multi_rows, coupled, living)


def draw_multi_index(key, part):
    return slot_layout(key)[0]


def draw_coupled_slot(key, part):
    return slot_layout(key)[1]


def draw_forcing(key, part):
    living = slot_layout(key)[2]
    noise_key = jax.random.fold_in(key, 23)
    columns = jnp.arange(COLUMNS, dtype=jnp.float32)[None, :, None] / COLUMNS
    slotted = jnp.arange(SLOTS, dtype=jnp.float32)[:, None, None] / SLOTS
    scaling = jnp.exp(jnp.log(3.0) * (columns + slotted)) / 3.0
    values = jnp.clip(jax.random.normal(noise_key, (SLOTS, COLUMNS, ROWS), jnp.float32), -4.0, 4.0) * scaling
    return jnp.where(living[:, None, None], values, 0.0)


def draw_start_guess(key, part):
    living = slot_layout(key)[2]
    noise_key = jax.random.fold_in(key, 29)
    values = 0.5 * jnp.clip(jax.random.normal(noise_key, (SLOTS, COLUMNS, ROWS), jnp.float32), -4.0, 4.0)
    return jnp.where(living[:, None, None], values, 0.0)


def shard_levels(stream_key, shape, pieces, smallest, top_value):
    factor_of = 1.0
    for dim, parts in pieces:
        steps = jax.random.uniform(jax.random.fold_in(jax.random.fold_in(stream_key, 6), dim), (parts,), jnp.float32, smallest / len(pieces), top_value / len(pieces))
        factor_of = factor_of * jnp.repeat(jnp.exp(steps), shape[dim] // parts).reshape((-1,) + (1,) * (len(shape) - 1 - dim))
    return factor_of


def setup_inputs(seed: int = 0) -> dict:
    keys = jax.random.split(jax.random.key(seed), 7)
    forcing = draw_forcing(jax.random.fold_in(keys[6], 71), 0)
    start_guess = draw_start_guess(jax.random.fold_in(keys[6], 71), 0)
    mean_field = jnp.clip(jnp.exp(math.log(2.0) - 0.6931472 * jax.random.uniform(keys[2], (COLUMNS, ROWS), jnp.float32) ** shard_levels(keys[2], (COLUMNS, ROWS), ((0, 8),), -0.2, 0.2)), 1.0, 2.0)
    mode_fields = jnp.clip(jax.random.uniform(keys[3], (MODES, COLUMNS, ROWS), jnp.float32, -0.04, 0.04) * shard_levels(keys[3], (MODES, COLUMNS, ROWS), ((1, 8),), -0.4, 0.0), -0.04, 0.04)
    multi_index = draw_multi_index(jax.random.fold_in(keys[6], 71), 0)
    coupled_slot = draw_coupled_slot(jax.random.fold_in(keys[6], 71), 0)
    return dict(forcing=forcing, start_guess=start_guess, mean_field=mean_field, mode_fields=mode_fields, multi_index=multi_index, coupled_slot=coupled_slot)


def stencil(values, coeffs):
    col_faces = 0.5 * (coeffs[1:] + coeffs[:-1])
    col_flux = col_faces * (values[:, 1:] - values[:, :-1])
    across = col_flux[:, :-1] - col_flux[:, 1:]
    inner_coef = jnp.pad(coeffs[1:-1], ((0, 0), (1, 1)))
    inner_vals = jnp.pad(values[:, 1:-1], ((0, 0), (0, 0), (1, 1)))
    row_faces = 0.5 * (inner_coef[:, 1:] + inner_coef[:, :-1])
    row_flux = row_faces * (inner_vals[:, :, 1:] - inner_vals[:, :, :-1])
    return across + row_flux[:, :, :-1] - row_flux[:, :, 1:]

def coupling(multi_index, coupled_slot, slot_count, mode_count):
    degrees = multi_index.astype(jnp.float32)
    raise_weight = jnp.where(coupled_slot[:, :mode_count] < slot_count, jnp.sqrt(degrees + 1.0), 0.0)
    lower_weight = jnp.sqrt(jnp.maximum(degrees, 0.0))
    raise_index = jnp.minimum(coupled_slot[:, :mode_count], slot_count - 1).astype(jnp.int32)
    lower_index = jnp.minimum(coupled_slot[:, mode_count:], slot_count - 1).astype(jnp.int32)
    return (raise_weight, lower_weight, raise_index, lower_index)

def operate(term_field, coeff_ext, raise_weight, lower_weight, raise_index, lower_index):
    extended = jnp.pad(term_field, ((0, 0), (1, 1), (0, 0)))
    result = stencil(extended, coeff_ext[0])
    for kl_mode in range(MODES):
        mixture = raise_weight[:, kl_mode, None, None] * extended[raise_index[:, kl_mode]]
        mixture = mixture + lower_weight[:, kl_mode, None, None] * extended[lower_index[:, kl_mode]]
        result = result + stencil(mixture, coeff_ext[kl_mode + 1])
    return result

def reference(forcing, start_guess, mean_field, mode_fields, multi_index, coupled_slot):
    raise_weight, lower_weight, raise_index, lower_index = coupling(multi_index, coupled_slot, SLOTS, MODES)
    stacked = jnp.concatenate([mean_field[None], mode_fields], axis=0)
    coeff_ext = jnp.pad(stacked, ((0, 0), (1, 1), (0, 0)))

    def apply_op(term_field):
        return operate(term_field, coeff_ext, raise_weight, lower_weight, raise_index, lower_index)
    approximation = start_guess
    residual = forcing - apply_op(start_guess)
    direction = residual
    norm_now = jnp.sum(residual * residual)
    for number in range(ITERS):
        applied = apply_op(direction)
        step_length = norm_now / jnp.sum(direction * applied)
        approximation = approximation + step_length * direction
        residual = residual - step_length * applied
        if number + 1 < ITERS:
            norm_next = jnp.sum(residual * residual)
            direction = residual + norm_next / norm_now * direction
            norm_now = norm_next
    return (approximation, residual)
```

```python
import functools
import math

import jax
import jax.numpy as jnp
import numpy as np
from jax import lax
from jax.experimental import pallas as pl
from jax.experimental.pallas import tpu as pltpu
from jax.sharding import PartitionSpec as P

DEGREE = 3
SUB = 8
LANES = 128
VMEM = pltpu.CompilerParams(vmem_limit_bytes=48 * 1024 * 1024)


def term_list(modes):
    triples = [
        (a, b, c) for a in range(modes + 1) for b in range(a + 1) for c in range(b + 1)
    ]
    place = {t: i for i, t in enumerate(triples)}
    edges = []
    for t in triples:
        used = [x for x in t if x]
        mine = []
        for k in range(1, modes + 1):
            power = used.count(k)
            if len(used) < DEGREE:
                up = tuple(sorted(used + [k], reverse=True))
                mine.append((place[up + (0,) * (DEGREE - len(up))], k - 1, power + 1))
            if power:
                left = list(used)
                left.remove(k)
                mine.append((place[tuple(left) + (0,) * (DEGREE - len(left))], k - 1, power))
        edges.append(mine)
    return edges


def rank_of(multi_index):
    modes = multi_index.shape[1]
    from_top = jnp.asarray(np.tril(np.ones((modes, modes), np.int32)))
    above = jnp.sum(jnp.maximum(multi_index, 0)[:, :, None] * from_top[None], axis=1)
    a, b, c = (jnp.sum((above >= n).astype(jnp.int32), axis=1) for n in (1, 2, 3))
    rank = a * (a + 1) * (a + 2) // 6 + b * (b + 1) // 2 + c
    return jnp.where(multi_index[:, 0] < 0, math.comb(modes + DEGREE, DEGREE), rank)


def columns_at(value, start, width):
    return lax.dynamic_slice_in_dim(value, start, width, axis=1)


def lane_next(u):
    lane = lax.broadcasted_iota(jnp.int32, u.shape, u.ndim - 1)
    return jnp.where(lane == LANES - 1, 0.0, pltpu.roll(u, LANES - 1, u.ndim - 1))


def lane_before(u):
    lane = lax.broadcasted_iota(jnp.int32, u.shape, u.ndim - 1)
    return jnp.where(lane == 0, 0.0, pltpu.roll(u, 1, u.ndim - 1))


def face_coefficients(coef_ref):
    east, right, left = [], [], []
    for k in range(coef_ref.shape[0]):
        c = coef_ref[k]
        east.append(0.5 * (c + pltpu.roll(c, SUB - 1, 0)))
        right.append(0.5 * (c + lane_next(c)))
        left.append(0.5 * (c + lane_before(c)))
    return east, right, left


def apply_operator(u_ref, coef_ref, edges, store, diff_ref):
    terms = len(edges)

    def differences(s, carry):
        u = u_ref[s]
        diff_ref[0, s] = pltpu.roll(u, SUB - 1, 0) - u
        diff_ref[1, s] = u - lane_next(u)
        diff_ref[2, s] = u - lane_before(u)
        return carry

    lax.fori_loop(0, terms, differences, 0, unroll=2)
    east, right, left = face_coefficients(coef_ref)
    for s in range(terms):
        groups = {1: [(s, 0)]}
        for t, k, weight in edges[s]:
            groups.setdefault(weight, []).append((t, k + 1))
        across = along = None
        for weight, members in groups.items():
            e = a = None
            for t, k in members:
                de = east[k] * diff_ref[0, t]
                da = right[k] * diff_ref[1, t] + left[k] * diff_ref[2, t]
                e = de if e is None else e + de
                a = da if a is None else a + da
            if weight > 1:
                e, a = e * math.sqrt(weight), a * math.sqrt(weight)
            across = e if across is None else across + e
            along = a if along is None else along + a
        store(s, pltpu.roll(across, 1, 0) - across + along)


def pack_rows(ranks_ref, packed_refs, field_ref, columns):
    per = SUB // columns
    rows = packed_refs[0].shape[0]
    sub = lax.broadcasted_iota(jnp.int32, (SUB, LANES), 0)
    for d, out in enumerate(packed_refs):

        def one(q, carry, d=d, out=out):
            row = field_ref[ranks_ref[(d * rows + q) * per]]
            for g in range(1, per):
                other = field_ref[ranks_ref[(d * rows + q) * per + g]]
                row = jnp.where(sub < g * columns, row, pltpu.roll(other, g * columns, 0))
            out[q] = row
            return carry

        lax.fori_loop(0, rows, one, 0, unroll=4)


def scatter_row(ranks_ref, at, row, field_ref, columns):
    per = SUB // columns
    for g in range(per):
        part = row if g == 0 else pltpu.roll(row, SUB - g * columns, 0)
        field_ref[ranks_ref[at * per + g], 0:columns] = part[0:columns]


def take_column(flat_ref, j, rows):
    return flat_ref[pl.ds(j, rows, stride=SUB), :]


def enter_kernel(n, columns, ranks_ref, *refs):
    parts, (field_ref, first_ref, last_ref) = refs[:n], refs[n:]
    rows = parts[0].shape[0]
    slots = field_ref.shape[0]
    field_ref[...] = jnp.zeros_like(field_ref)
    for d, part in enumerate(parts):

        def one(q, carry, d=d, part=part):
            scatter_row(ranks_ref, d * rows + q, part[q], field_ref, columns)
            return carry

        lax.fori_loop(0, rows, one, 0, unroll=4)
    flat = field_ref.reshape(slots * SUB, LANES)
    first_ref[...] = take_column(flat, 0, slots)
    last_ref[...] = take_column(flat, columns - 1, slots)


def start_kernel(n, columns, edges, ranks_ref, x_ref, before_ref, after_ref, coef_ref, *refs):
    packed, (u_ref, y_ref, diff_ref) = refs[:n], refs[n:]
    slots = x_ref.shape[0]
    u_ref[...] = x_ref[...]
    flat = u_ref.reshape(slots * SUB, LANES)
    flat[pl.ds(SUB - 1, slots, stride=SUB), :] = before_ref[...]
    flat[pl.ds(columns, slots, stride=SUB), :] = after_ref[...]
    y_ref[len(edges) :] = jnp.zeros((slots - len(edges), SUB, LANES), jnp.float32)

    def store(s, value):
        y_ref[s] = value

    apply_operator(u_ref, coef_ref, edges, store, diff_ref)
    pack_rows(ranks_ref, packed, y_ref, columns)


def residual_kernel(n, columns, ranks_ref, *refs):
    forcing, image = refs[:n], refs[n : 2 * n]
    packed = refs[2 * n : 3 * n]
    field_ref, first_ref, last_ref, sum_ref = refs[3 * n :]
    rows = forcing[0].shape[0]
    slots = field_ref.shape[0]
    field_ref[...] = jnp.zeros_like(field_ref)
    total = jnp.zeros((SUB, LANES), jnp.float32)
    for d in range(n):

        def one(q, total, d=d):
            v = forcing[d][q] - image[d][q]
            packed[d][q] = v
            scatter_row(ranks_ref, d * rows + q, v, field_ref, columns)
            return total + v * v

        total = lax.fori_loop(0, rows, one, total, unroll=4)
    sum_ref[...] = total
    flat = field_ref.reshape(slots * SUB, LANES)
    for j in range(2):
        first_ref[j] = take_column(flat, j, slots)
        last_ref[j] = take_column(flat, columns - 2 + j, slots)


def first_kernel(n, columns, edges, ranks_ref, v_ref, before_ref, after_ref, coef_ref, inside_ref, *refs):
    packed, (out_ref, sum_ref), (u_ref, diff_ref) = refs[:n], refs[n : n + 2], refs[n + 2 :]
    slots = v_ref.shape[0]
    u_ref[...] = v_ref[...]
    flat = u_ref.reshape(slots * SUB, LANES)
    for j in range(2):
        flat[pl.ds(SUB - 2 + j, slots, stride=SUB), :] = before_ref[j]
        flat[pl.ds(columns + j, slots, stride=SUB), :] = after_ref[j]
    out_ref[len(edges) :] = jnp.zeros((slots - len(edges), SUB, LANES), jnp.float32)
    inside = inside_ref[...] > 0.0

    def store(s, value):
        out_ref[s] = jnp.where(inside, value, 0.0)

    apply_operator(u_ref, coef_ref, edges, store, diff_ref)
    own = lax.broadcasted_iota(jnp.int32, (SUB, LANES), 0) < columns

    def dot(s, total):
        return total + jnp.where(own, u_ref[s] * out_ref[s], 0.0)

    sum_ref[...] = lax.fori_loop(0, len(edges), dot, jnp.zeros((SUB, LANES), jnp.float32), unroll=4)
    pack_rows(ranks_ref, packed, out_ref, columns)


def second_kernel(n, columns, edges, ranks_ref, v_ref, coef_ref, *refs):
    packed, (y_ref, diff_ref) = refs[:n], refs[n:]
    slots = v_ref.shape[0]
    y_ref[len(edges) :] = jnp.zeros((slots - len(edges), SUB, LANES), jnp.float32)

    def store(s, value):
        y_ref[s] = value

    apply_operator(v_ref, coef_ref, edges, store, diff_ref)
    pack_rows(ranks_ref, packed, y_ref, columns)


def lines_of(sums_ref, count):
    full = jnp.sum(sums_ref[...], axis=1, keepdims=True)
    return [full[i : i + 1] for i in range(count)]


def dots_kernel(n, sums_ref, *refs):
    v0, v1, v2, out_ref = refs[:n], refs[n : 2 * n], refs[2 * n : 3 * n], refs[3 * n]
    rows = v0[0].shape[0]
    s00, s01 = lines_of(sums_ref, 2)
    step = s00 / s01
    totals = (jnp.zeros((SUB, LANES), jnp.float32),) * 4
    for d in range(n):

        def one(q, totals, d=d):
            a, b, c = v0[d][q], v1[d][q], v2[d][q]
            r = a - step * b
            image = b - step * c
            return tuple(t + x for t, x in zip(totals, (r * r, r * image, r * b, a * image)))

        totals = lax.fori_loop(0, rows, one, totals, unroll=4)
    out_ref[...] = jnp.zeros_like(out_ref)
    for i, t in enumerate(totals):
        out_ref[i : i + 1] = jnp.sum(t, axis=0, keepdims=True)


def finish_kernel(n, columns, offsets_ref, first_ref, second_ref, x_ref, f_ref, *refs):
    image, v1, v2 = refs[:n], refs[n : 2 * n], refs[2 * n : 3 * n]
    approx_ref, residual_ref = refs[3 * n :]
    per = SUB // columns
    rows = image[0].shape[0]
    s00, s01 = lines_of(first_ref, 2)
    rr, r_ar, r_v1, v0_ar = lines_of(second_ref, 4)
    step = s00 / s01
    beta = rr / s00
    last = rr / (r_ar + beta * (r_v1 + v0_ar) + beta * beta * s01)
    whole = step + last * beta
    for d in range(n):
        at = pl.ds(pl.multiple_of(offsets_ref[d], columns), columns)

        def one(q, carry, d=d, at=at):
            y, b, c = image[d][q], v1[d][q], v2[d][q]
            for g in range(per):
                part = slice(g * columns, (g + 1) * columns)
                s = q * per + g
                yg, bg, cg = y[part], b[part], c[part]
                v0 = f_ref[s, at] - yg
                r1 = v0 - step * bg
                approx_ref[s, at] = x_ref[s, at] + whole * v0 + last * r1
                residual_ref[s, at] = r1 - last * ((1.0 + beta) * bg - step * cg)
            return carry

        lax.fori_loop(0, rows, one, 0, unroll=2)


def call(kernel, scalars, arrays, outs, scratch=()):
    whole = pl.BlockSpec(memory_space=pltpu.VMEM)
    return pl.pallas_call(
        kernel,
        in_specs=[pl.BlockSpec(memory_space=pltpu.SMEM)] * len(scalars) + [whole] * len(arrays),
        out_specs=[whole] * len(outs),
        out_shape=[jax.ShapeDtypeStruct(s, jnp.float32) for s in outs],
        scratch_shapes=[pltpu.VMEM(s, jnp.float32) for s in scratch],
        compiler_params=VMEM,
    )(*scalars, *arrays)


def butterfly(value, sizes):
    count = math.prod(sizes)
    bit = 1
    while bit < count:
        value = value + lax.ppermute(value, ("space", "chaos"), [(i, i ^ bit) for i in range(count)])
        bit *= 2
    return value


def per_device(forcing, start_guess, mean_field, mode_fields, multi_index, coupled_slot):
    spaces, n = lax.axis_size("space"), lax.axis_size("chaos")
    i, z = lax.axis_index("space"), lax.axis_index("chaos")
    here, width, lanes = forcing.shape
    modes = mode_fields.shape[0]
    columns = width // n
    rows = here * columns // SUB
    slots = n * here
    edges = term_list(modes)

    def chunk(space, chaos):
        return jnp.where(space % 2 == 0, chaos, n - 1 - chaos)

    def device_at(p):
        tile, c = divmod(p, n)
        return tile * n + (c if tile % 2 == 0 else n - 1 - c)

    line = [(device_at(p), device_at(p + 1)) for p in range(spaces * n - 1)]
    back_line = [(b, a) for a, b in line]
    both = ("space", "chaos")

    def outward(d):
        return [(j, (j + d) % n) for j in range(n)]

    def homeward(d):
        return [(j, (j - d) % n) for j in range(n)]

    offsets = [columns * chunk(i, (z + d) % n) for d in range(n)]

    def cut(value, d):
        return columns_at(value, offsets[d], columns).reshape(rows, SUB, lanes)

    def sent(parts, way):
        return parts[:1] + [lax.ppermute(parts[d], "chaos", way(d)) for d in range(1, n)]

    rank = rank_of(multi_index)
    tag = jnp.pad(rank.astype(jnp.float32)[None, None], ((0, 0), (0, SUB - 1), (0, lanes - here)))
    x_parts = sent([jnp.concatenate([cut(start_guess, d), tag], axis=0) for d in range(n)], outward)
    ranks = jnp.concatenate([p[rows, 0, :here] for p in x_parts]).astype(jnp.int32)
    x_parts = [p[:rows] for p in x_parts]
    f_parts = sent([cut(forcing, d) for d in range(n)], outward)

    stacked = jnp.concatenate([mean_field[None], mode_fields], axis=0)
    up = [(j, j + 1) for j in range(spaces - 1)]
    down = [(j + 1, j) for j in range(spaces - 1)]
    coef = jnp.concatenate(
        [
            lax.ppermute(stacked[:, width - 2 :], "space", up),
            stacked,
            lax.ppermute(stacked[:, :2], "space", down),
        ],
        axis=1,
    )
    coef = columns_at(coef, offsets[0], columns + 4)
    gap = jnp.zeros((modes + 1, SUB - columns - 4, lanes), jnp.float32)
    coef = jnp.concatenate([coef[:, 2:], gap, coef[:, :2]], axis=1)
    sub = lax.broadcasted_iota(jnp.int32, (SUB, lanes), 0)
    position = i * n + chunk(i, z)
    outside = ((position == 0) & (sub >= SUB - 2)) | (
        (position == spaces * n - 1) & (sub >= columns) & (sub < columns + 2)
    )
    inside = jnp.where(outside, 0.0, 1.0)

    field, part, small = (slots, SUB, lanes), (rows, SUB, lanes), (SUB, lanes)
    diff = (3,) + field

    x, x_first, x_last = call(
        functools.partial(enter_kernel, n, columns),
        [ranks],
        x_parts,
        [field, (slots, lanes), (slots, lanes)],
    )
    x_before = lax.ppermute(x_last, both, line)
    x_after = lax.ppermute(x_first, both, back_line)
    image = call(
        functools.partial(start_kernel, n, columns, edges),
        [ranks],
        [x, x_before, x_after, coef],
        [part] * n,
        [field, field, diff],
    )
    *v0_parts, v0, v0_first, v0_last, sum00 = call(
        functools.partial(residual_kernel, n, columns),
        [ranks],
        f_parts + list(image),
        [part] * n + [field, (2, slots, lanes), (2, slots, lanes), small],
    )
    v0_before = lax.ppermute(v0_last, both, line)
    v0_after = lax.ppermute(v0_first, both, back_line)
    image_home = sent(list(image), homeward)
    *v1_parts, v1, sum01 = call(
        functools.partial(first_kernel, n, columns, edges),
        [ranks],
        [v0, v0_before, v0_after, coef, inside],
        [part] * n + [field, small],
        [field, diff],
    )
    v1_home = sent(v1_parts, homeward)
    sums = jnp.stack([jnp.sum(sum00, axis=0), jnp.sum(sum01, axis=0)])
    sums = butterfly(jnp.pad(sums, ((0, SUB - 2), (0, 0))), (spaces, n))
    v2_parts = call(
        functools.partial(second_kernel, n, columns, edges),
        [ranks],
        [v1, coef],
        [part] * n,
        [field, diff],
    )
    v2_home = sent(list(v2_parts), homeward)
    (dots,) = call(
        functools.partial(dots_kernel, n),
        [],
        [sums] + v0_parts + v1_parts + list(v2_parts),
        [small],
    )
    dots = butterfly(dots, (spaces, n))
    return call(
        functools.partial(finish_kernel, n, columns),
        [jnp.stack(offsets).astype(jnp.int32)],
        [sums, dots, start_guess, forcing] + image_home + v1_home + v2_home,
        [forcing.shape] * 2,
    )


def solution(mesh):
    placed = (
        P("chaos", "space", None),
        P("chaos", "space", None),
        P("space", None),
        P(None, "space", None),
        P("chaos", None),
        P("chaos", None),
    )
    return jax.shard_map(
        lambda *a: tuple(per_device(*a)),
        mesh=mesh,
        in_specs=placed,
        out_specs=(P("chaos", "space", None), P("chaos", "space", None)),
        check_vma=False,
    )
```

```python
import functools
import math

import jax
import jax.numpy as jnp
import numpy as np
from jax import lax
from jax.experimental import pallas as pl
from jax.experimental.pallas import tpu as pltpu
from jax.sharding import PartitionSpec as P

DEGREE = 3
SUB = 8
LANES = 128
PARAMS = pltpu.CompilerParams(vmem_limit_bytes=24 * 1024 * 1024)


def term_list(modes):
    triples = [
        (a, b, c) for a in range(modes + 1) for b in range(a + 1) for c in range(b + 1)
    ]
    place = {t: i for i, t in enumerate(triples)}
    edges = []
    for t in triples:
        used = [x for x in t if x]
        mine = []
        for k in range(1, modes + 1):
            power = used.count(k)
            if len(used) < DEGREE:
                up = tuple(sorted(used + [k], reverse=True))
                mine.append((place[up + (0,) * (DEGREE - len(up))], k - 1, power + 1))
            if power:
                left = list(used)
                left.remove(k)
                mine.append((place[tuple(left) + (0,) * (DEGREE - len(left))], k - 1, power))
        edges.append(mine)
    return edges


def rank_of(multi_index):
    modes = multi_index.shape[1]
    from_top = jnp.asarray(np.tril(np.ones((modes, modes), np.int32)))
    above = jnp.sum(jnp.maximum(multi_index, 0)[:, :, None] * from_top[None], axis=1)
    a, b, c = (jnp.sum((above >= n).astype(jnp.int32), axis=1) for n in (1, 2, 3))
    rank = a * (a + 1) * (a + 2) // 6 + b * (b + 1) // 2 + c
    return jnp.where(multi_index[:, 0] < 0, math.comb(modes + DEGREE, DEGREE), rank)


def columns_at(value, start, width):
    return lax.dynamic_slice_in_dim(value, start, width, axis=1)


def lane_next(u):
    lane = lax.broadcasted_iota(jnp.int32, u.shape, u.ndim - 1)
    return jnp.where(lane == LANES - 1, 0.0, pltpu.roll(u, LANES - 1, u.ndim - 1))


def lane_before(u):
    lane = lax.broadcasted_iota(jnp.int32, u.shape, u.ndim - 1)
    return jnp.where(lane == 0, 0.0, pltpu.roll(u, 1, u.ndim - 1))


def face_coefficients(coef_ref):
    east, right, left = [], [], []
    for k in range(coef_ref.shape[0]):
        c = coef_ref[k]
        east.append(0.5 * (c + pltpu.roll(c, SUB - 1, 0)))
        right.append(0.5 * (c + lane_next(c)))
        left.append(0.5 * (c + lane_before(c)))
    return east, right, left


def apply_operator(u_ref, coef_ref, edges, store, diff_ref):
    terms = len(edges)

    u = u_ref[0:terms]
    diff_ref[0, 0:terms] = pltpu.roll(u, SUB - 1, 1) - u
    diff_ref[1, 0:terms] = u - lane_next(u)
    diff_ref[2, 0:terms] = u - lane_before(u)
    east, right, left = face_coefficients(coef_ref)
    for s in range(terms):
        groups = {1: [(s, 0)]}
        for t, k, weight in edges[s]:
            groups.setdefault(weight, []).append((t, k + 1))
        across = along = None
        for weight, members in groups.items():
            e = a = None
            for t, k in members:
                de = east[k] * diff_ref[0, t]
                da = right[k] * diff_ref[1, t] + left[k] * diff_ref[2, t]
                e = de if e is None else e + de
                a = da if a is None else a + da
            if weight > 1:
                e, a = e * math.sqrt(weight), a * math.sqrt(weight)
            across = e if across is None else across + e
            along = a if along is None else along + a
        store(s, pltpu.roll(across, 1, 0) - across + along)


def pack_rows(ranks_ref, packed_refs, field_ref, columns):
    per = SUB // columns
    rows = packed_refs[0].shape[0]
    sub = lax.broadcasted_iota(jnp.int32, (SUB, LANES), 0)
    for d, out in enumerate(packed_refs):

        def one(q, carry, d=d, out=out):
            row = field_ref[ranks_ref[(d * rows + q) * per]]
            for g in range(1, per):
                other = field_ref[ranks_ref[(d * rows + q) * per + g]]
                row = jnp.where(sub < g * columns, row, pltpu.roll(other, g * columns, 0))
            out[q] = row
            return carry

        lax.fori_loop(0, rows, one, 0, unroll=4)


def scatter_row(ranks_ref, at, row, field_ref, columns):
    per = SUB // columns
    for g in range(per):
        part = row if g == 0 else pltpu.roll(row, SUB - g * columns, 0)
        field_ref[ranks_ref[at * per + g], 0:columns] = part[0:columns]


def take_column(flat_ref, j, rows):
    return flat_ref[pl.ds(j, rows, stride=SUB), :]


def enter_kernel(n, columns, rows, ranks_ref, coef_ref, *refs):
    parts, (field_ref, first_ref, last_ref) = refs[:n], refs[n:]
    slots = field_ref.shape[0]
    fields = coef_ref.shape[0]
    field_ref[...] = jnp.zeros_like(field_ref)
    for d, part in enumerate(parts):

        def one(q, carry, d=d, part=part):
            scatter_row(ranks_ref, d * rows + q, part[q], field_ref, columns)
            return carry

        lax.fori_loop(0, rows, one, 0, unroll=4)
    flat = field_ref.reshape(slots * SUB, LANES)
    first_ref[slots:] = jnp.zeros_like(first_ref[slots:])
    last_ref[slots:] = jnp.zeros_like(last_ref[slots:])
    first_ref[0:slots] = take_column(flat, 0, slots)
    last_ref[0:slots] = take_column(flat, columns - 1, slots)
    flat = coef_ref.reshape(fields * SUB, LANES)
    for j in range(2):
        at = slots + j * fields
        first_ref[at : at + fields] = take_column(flat, j, fields)
        last_ref[at : at + fields] = take_column(flat, columns - 2 + j, fields)


def start_kernel(n, columns, edges, ranks_ref, x_ref, before_ref, after_ref, own_ref, *refs):
    packed, (coef_ref, u_ref, y_ref, diff_ref) = refs[:n], refs[n:]
    slots, fields = x_ref.shape[0], own_ref.shape[0]
    coef_ref[...] = own_ref[...]
    flat = coef_ref.reshape(fields * SUB, LANES)
    for j in range(2):
        at = slots + j * fields
        flat[pl.ds(SUB - 2 + j, fields, stride=SUB), :] = before_ref[at : at + fields]
        flat[pl.ds(columns + j, fields, stride=SUB), :] = after_ref[at : at + fields]
    u_ref[...] = x_ref[...]
    flat = u_ref.reshape(slots * SUB, LANES)
    flat[pl.ds(SUB - 1, slots, stride=SUB), :] = before_ref[0:slots]
    flat[pl.ds(columns, slots, stride=SUB), :] = after_ref[0:slots]
    y_ref[len(edges) :] = jnp.zeros((slots - len(edges), SUB, LANES), jnp.float32)

    def store(s, value):
        y_ref[s] = value

    apply_operator(u_ref, coef_ref, edges, store, diff_ref)
    pack_rows(ranks_ref, packed, y_ref, columns)


def residual_kernel(n, columns, ranks_ref, *refs):
    forcing, image = refs[:n], refs[n : 2 * n]
    packed = refs[2 * n : 3 * n]
    field_ref, first_ref, last_ref = refs[3 * n :]
    rows = forcing[0].shape[0]
    slots = field_ref.shape[0]
    field_ref[...] = jnp.zeros_like(field_ref)
    for d in range(n):

        def one(q, carry, d=d):
            v = forcing[d][q] - image[d][q]
            packed[d][q] = v
            scatter_row(ranks_ref, d * rows + q, v, field_ref, columns)
            return carry

        lax.fori_loop(0, rows, one, 0, unroll=4)
    flat = field_ref.reshape(slots * SUB, LANES)
    for j in range(2):
        first_ref[j] = take_column(flat, j, slots)
        last_ref[j] = take_column(flat, columns - 2 + j, slots)


def first_kernel(n, columns, edges, ranks_ref, v_ref, before_ref, after_ref, coef_ref, inside_ref, *refs):
    packed, (out_ref, u_ref, diff_ref) = refs[:n], refs[n:]
    slots = v_ref.shape[0]
    u_ref[...] = v_ref[...]
    flat = u_ref.reshape(slots * SUB, LANES)
    for j in range(2):
        flat[pl.ds(SUB - 2 + j, slots, stride=SUB), :] = before_ref[j]
        flat[pl.ds(columns + j, slots, stride=SUB), :] = after_ref[j]
    out_ref[len(edges) :] = jnp.zeros((slots - len(edges), SUB, LANES), jnp.float32)
    inside = inside_ref[...] > 0.0

    def store(s, value):
        out_ref[s] = jnp.where(inside, value, 0.0)

    apply_operator(u_ref, coef_ref, edges, store, diff_ref)
    pack_rows(ranks_ref, packed, out_ref, columns)


def second_kernel(n, columns, edges, ranks_ref, v_ref, coef_ref, *refs):
    packed, (y_ref, diff_ref) = refs[:n], refs[n:]
    slots = v_ref.shape[0]
    y_ref[len(edges) :] = jnp.zeros((slots - len(edges), SUB, LANES), jnp.float32)

    def store(s, value):
        y_ref[s] = value

    apply_operator(v_ref, coef_ref, edges, store, diff_ref)
    pack_rows(ranks_ref, packed, y_ref, columns)


def row_sums(n, rows, of_row, count):
    totals = (jnp.zeros((SUB, LANES), jnp.float32),) * count
    for d in range(n):

        def one(q, totals, d=d):
            return tuple(t + x for t, x in zip(totals, of_row(d, q)))

        totals = lax.fori_loop(0, rows, one, totals, unroll=4)
    return [jnp.sum(jnp.sum(t, axis=0, keepdims=True), axis=1, keepdims=True) for t in totals]


def dots_kernel(n, place_ref, *refs):
    v0, v1, v2, out_ref = refs[:n], refs[n : 2 * n], refs[2 * n : 3 * n], refs[3 * n]
    rows = v0[0].shape[0]
    aa, ab = row_sums(n, rows, lambda d, q: (v0[d][q] * v0[d][q], v0[d][q] * v1[d][q]), 2)
    m = jnp.where(aa > 0.0, ab / jnp.where(aa > 0.0, aa, 1.0), 0.0)

    def products(d, q):
        a, b, c = v0[d][q], v1[d][q], v2[d][q]
        w = b - m * a
        e = c - m * b
        return a * w, w * w, a * e, w * b, w * e

    entries = [aa, ab, m] + row_sums(n, rows, products, 5)
    lane = lax.broadcasted_iota(jnp.int32, out_ref.shape, 1)
    row = lax.broadcasted_iota(jnp.int32, out_ref.shape, 0)
    table = jnp.zeros(out_ref.shape, jnp.float32)
    for k, value in enumerate(entries):
        table = jnp.where(lane == k, value, table)
    out_ref[...] = jnp.where(row == place_ref[0], table, 0.0)


def step_lengths(table):
    lane = lax.broadcasted_iota(jnp.int32, table.shape, 1)
    aa, ab, m, aw, ww, ae, wb, we = (
        jnp.sum(jnp.where(lane == k, table, 0.0), axis=1, keepdims=True) for k in range(8)
    )

    def total(x):
        return jnp.sum(x, axis=0, keepdims=True)

    norm, curve = total(aa), total(ab)
    step = norm / curve
    g = 1.0 - step * m
    rr = total(g * g * aa - 2.0 * g * step * aw + step * step * ww)
    r_ar = total(g * g * ab - g * step * (ae + wb) + step * step * we)
    mixed = total(2.0 * g * ab - step * (wb + ae))
    beta = rr / norm
    return step, beta, rr / (r_ar + beta * mixed + beta * beta * curve)


def finish_kernel(n, columns, offsets_ref, table_ref, x_ref, f_ref, *refs):
    image, v1, v2 = refs[:n], refs[n : 2 * n], refs[2 * n : 3 * n]
    approx_ref, residual_ref = refs[3 * n :]
    per = SUB // columns
    rows = image[0].shape[0]
    step, beta, last = step_lengths(table_ref[...])
    whole = step + last * beta
    for d in range(n):
        at = pl.ds(pl.multiple_of(offsets_ref[d], columns), columns)

        def one(q, carry, d=d, at=at):
            y, b, c = image[d][q], v1[d][q], v2[d][q]
            for g in range(per):
                part = slice(g * columns, (g + 1) * columns)
                s = q * per + g
                yg, bg, cg = y[part], b[part], c[part]
                v0 = f_ref[s, at] - yg
                r1 = v0 - step * bg
                approx_ref[s, at] = x_ref[s, at] + whole * v0 + last * r1
                residual_ref[s, at] = r1 - last * ((1.0 + beta) * bg - step * cg)
            return carry

        lax.fori_loop(0, rows, one, 0, unroll=2)


def call(kernel, scalars, arrays, outs, scratch=()):
    whole = pl.BlockSpec(memory_space=pltpu.VMEM)
    return pl.pallas_call(
        kernel,
        in_specs=[pl.BlockSpec(memory_space=pltpu.SMEM)] * len(scalars) + [whole] * len(arrays),
        out_specs=[whole] * len(outs),
        out_shape=[jax.ShapeDtypeStruct(s, jnp.float32) for s in outs],
        scratch_shapes=[pltpu.VMEM(s, jnp.float32) for s in scratch],
        compiler_params=PARAMS,
    )(*scalars, *arrays)


def butterfly(value, sizes):
    count = math.prod(sizes)
    bit = 1
    while bit < count:
        value = value + lax.ppermute(value, ("space", "chaos"), [(i, i ^ bit) for i in range(count)])
        bit *= 2
    return value


def per_device(forcing, start_guess, mean_field, mode_fields, multi_index, coupled_slot):
    spaces, n = lax.axis_size("space"), lax.axis_size("chaos")
    i, z = lax.axis_index("space"), lax.axis_index("chaos")
    here, width, lanes = forcing.shape
    modes = mode_fields.shape[0]
    columns = width // n
    rows = here * columns // SUB
    slots = n * here
    edges = term_list(modes)

    def chunk(space, chaos):
        return jnp.where(space % 2 == 0, chaos, n - 1 - chaos)

    def device_at(p):
        tile, c = divmod(p, n)
        return tile * n + (c if tile % 2 == 0 else n - 1 - c)

    line = [(device_at(p), device_at(p + 1)) for p in range(spaces * n - 1)]
    back_line = [(b, a) for a, b in line]
    both = ("space", "chaos")

    def outward(d):
        return [(j, (j + d) % n) for j in range(n)]

    def homeward(d):
        return [(j, (j - d) % n) for j in range(n)]

    offsets = [columns * chunk(i, (z + d) % n) for d in range(n)]

    def cut(value, d):
        return columns_at(value, offsets[d], columns).reshape(rows, SUB, lanes)

    def sent(parts, way):
        return parts[:1] + [lax.ppermute(parts[d], "chaos", way(d)) for d in range(1, n)]

    rank = rank_of(multi_index)
    tag = jnp.pad(rank.astype(jnp.float32)[None, None], ((0, 0), (0, SUB - 1), (0, lanes - here)))
    x_parts = sent([jnp.concatenate([cut(start_guess, d), tag], axis=0) for d in range(n)], outward)
    ranks = jnp.concatenate([p[rows, 0, :here] for p in x_parts]).astype(jnp.int32)
    f_parts = sent([cut(forcing, d) for d in range(n)], outward)

    stacked = jnp.concatenate([mean_field[None], mode_fields], axis=0)
    own_coef = jnp.pad(columns_at(stacked, offsets[0], columns), ((0, 0), (0, SUB - columns), (0, 0)))
    sub = lax.broadcasted_iota(jnp.int32, (SUB, lanes), 0)
    position = i * n + chunk(i, z)
    outside = ((position == 0) & (sub >= SUB - 2)) | (
        (position == spaces * n - 1) & (sub >= columns) & (sub < columns + 2)
    )
    inside = jnp.where(outside, 0.0, 1.0)

    field, part, fields = (slots, SUB, lanes), (rows, SUB, lanes), (modes + 1, SUB, lanes)
    diff = (3,) + field
    edge = (-(-(slots + 2 * (modes + 1)) // SUB) * SUB, lanes)

    x, x_first, x_last = call(
        functools.partial(enter_kernel, n, columns, rows),
        [ranks],
        [own_coef] + x_parts,
        [field, edge, edge],
    )
    x_before = lax.ppermute(x_last, both, line)
    x_after = lax.ppermute(x_first, both, back_line)
    *image, coef = call(
        functools.partial(start_kernel, n, columns, edges),
        [ranks],
        [x, x_before, x_after, own_coef],
        [part] * n + [fields],
        [field, field, diff],
    )
    *v0_parts, v0, v0_first, v0_last = call(
        functools.partial(residual_kernel, n, columns),
        [ranks],
        f_parts + image,
        [part] * n + [field, (2, slots, lanes), (2, slots, lanes)],
    )
    v0_before = lax.ppermute(v0_last, both, line)
    v0_after = lax.ppermute(v0_first, both, back_line)
    image_home = sent(image, homeward)
    *v1_parts, v1 = call(
        functools.partial(first_kernel, n, columns, edges),
        [ranks],
        [v0, v0_before, v0_after, coef, inside],
        [part] * n + [field],
        [field, diff],
    )
    v1_home = sent(v1_parts, homeward)
    v2_parts = call(
        functools.partial(second_kernel, n, columns, edges),
        [ranks],
        [v1, coef],
        [part] * n,
        [field, diff],
    )
    v2_home = sent(list(v2_parts), homeward)
    (table,) = call(
        functools.partial(dots_kernel, n),
        [(i * n + z).astype(jnp.int32)[None]],
        v0_parts + v1_parts + list(v2_parts),
        [(-(-spaces * n // SUB) * SUB, lanes)],
    )
    table = butterfly(table, (spaces, n))
    return call(
        functools.partial(finish_kernel, n, columns),
        [jnp.stack(offsets).astype(jnp.int32)],
        [table, start_guess, forcing] + image_home + v1_home + v2_home,
        [forcing.shape] * 2,
    )


def solution(mesh):
    placed = (
        P("chaos", "space", None),
        P("chaos", "space", None),
        P("space", None),
        P(None, "space", None),
        P("chaos", None),
        P("chaos", None),
    )
    return jax.shard_map(
        lambda *a: tuple(per_device(*a)),
        mesh=mesh,
        in_specs=placed,
        out_specs=(P("chaos", "space", None), P("chaos", "space", None)),
        check_vma=False,
    )
```

```python
import functools
import math

import jax
import jax.numpy as jnp
import numpy as np
from jax import lax
from jax.experimental import pallas as pl
from jax.experimental.pallas import tpu as pltpu
from jax.sharding import PartitionSpec as P

DEGREE = 3
SUB = 8
LANES = 128
PARAMS = pltpu.CompilerParams(vmem_limit_bytes=12 * 1024 * 1024)


def term_list(modes):
    triples = [
        (a, b, c) for a in range(modes + 1) for b in range(a + 1) for c in range(b + 1)
    ]
    place = {t: i for i, t in enumerate(triples)}
    edges = []
    for t in triples:
        used = [x for x in t if x]
        mine = []
        for k in range(1, modes + 1):
            power = used.count(k)
            if len(used) < DEGREE:
                up = tuple(sorted(used + [k], reverse=True))
                mine.append((place[up + (0,) * (DEGREE - len(up))], k - 1, power + 1))
            if power:
                left = list(used)
                left.remove(k)
                mine.append((place[tuple(left) + (0,) * (DEGREE - len(left))], k - 1, power))
        edges.append(mine)
    return edges


def rank_row(multi_index):
    here, modes = multi_index.shape
    above = jnp.zeros((here, 1), jnp.int32)
    symbols = [jnp.zeros((here, 1), jnp.int32)] * DEGREE
    for k in reversed(range(modes)):
        above += jnp.maximum(multi_index[:, k : k + 1], 0)
        symbols = [a + jnp.where(above > n, 1, 0) for n, a in enumerate(symbols)]
    a, b, c = symbols
    rank = a * (a + 1) * (a + 2) // 6 + b * (b + 1) // 2 + c
    rank = jnp.where(multi_index[:, 0:1] < 0, math.comb(modes + DEGREE, DEGREE), rank).astype(jnp.float32)
    lane = lax.broadcasted_iota(jnp.int32, (here, LANES), 1)
    slot = lax.broadcasted_iota(jnp.int32, (here, LANES), 0)
    return jnp.sum(jnp.where(lane == slot, rank, 0.0), axis=0, keepdims=True)


def cut_kernel(n, columns, rows, offsets_ref, source_ref, *refs):
    per = SUB // columns
    index, parts = refs[:-n], refs[-n:]
    for d, out in enumerate(parts):
        at = pl.ds(pl.multiple_of(offsets_ref[d], columns), columns)
        for g in range(per):
            for q in range(rows):
                out[q, g * columns : (g + 1) * columns] = source_ref[q * per + g, at]
    if index:
        first = lax.broadcasted_iota(jnp.int32, (SUB, LANES), 0) == 0
        tag = jnp.where(first, rank_row(index[0][...]), 0.0)
        for out in parts:
            out[rows] = tag


def lane_next(u):
    lane = lax.broadcasted_iota(jnp.int32, u.shape, u.ndim - 1)
    return jnp.where(lane == LANES - 1, 0.0, pltpu.roll(u, LANES - 1, u.ndim - 1))


def lane_before(u):
    lane = lax.broadcasted_iota(jnp.int32, u.shape, u.ndim - 1)
    return jnp.where(lane == 0, 0.0, pltpu.roll(u, 1, u.ndim - 1))


def face_coefficients(coef_ref):
    east, right, left = [], [], []
    for k in range(coef_ref.shape[0]):
        c = coef_ref[k]
        east.append(0.5 * (c + pltpu.roll(c, SUB - 1, 0)))
        right.append(0.5 * (c + lane_next(c)))
        left.append(0.5 * (c + lane_before(c)))
    return east, right, left


def apply_operator(u_ref, coef_ref, edges, store, diff_ref):
    terms = len(edges)

    u = u_ref[0:terms]
    diff_ref[0, 0:terms] = pltpu.roll(u, SUB - 1, 1) - u
    diff_ref[1, 0:terms] = u - lane_next(u)
    diff_ref[2, 0:terms] = u - lane_before(u)
    east, right, left = face_coefficients(coef_ref)
    for s in range(terms):
        groups = {1: [(s, 0)]}
        for t, k, weight in edges[s]:
            groups.setdefault(weight, []).append((t, k + 1))
        across = along = None
        for weight, members in groups.items():
            e = a = None
            for t, k in members:
                de = east[k] * diff_ref[0, t]
                da = right[k] * diff_ref[1, t] + left[k] * diff_ref[2, t]
                e = de if e is None else e + de
                a = da if a is None else a + da
            if weight > 1:
                e, a = e * math.sqrt(weight), a * math.sqrt(weight)
            across = e if across is None else across + e
            along = a if along is None else along + a
        store(s, pltpu.roll(across, 1, 0) - across + along)


def pack_rows(ranks_ref, packed_refs, field_ref, columns, rows, first=0):
    per = SUB // columns
    sub = lax.broadcasted_iota(jnp.int32, (SUB, LANES), 0)
    for d, out in enumerate(packed_refs):

        def one(q, carry, d=d, out=out):
            row = field_ref[ranks_ref[(d * rows + q) * per]]
            for g in range(1, per):
                other = field_ref[ranks_ref[(d * rows + q) * per + g]]
                row = jnp.where(sub < g * columns, row, pltpu.roll(other, g * columns, 0))
            out[first + q] = row
            return carry

        lax.fori_loop(0, rows, one, 0, unroll=4)


def scatter_row(ranks_ref, at, row, field_ref, columns):
    per = SUB // columns
    for g in range(per):
        part = row if g == 0 else pltpu.roll(row, SUB - g * columns, 0)
        field_ref[ranks_ref[at * per + g], 0:columns] = part[0:columns]


def take_column(flat_ref, j, rows):
    return flat_ref[pl.ds(j, rows, stride=SUB), :]


def enter_kernel(n, columns, rows, ranks_ref, coef_ref, _, *refs):
    parts, (field_ref, first_ref, last_ref) = refs[:n], refs[n:]
    slots = field_ref.shape[0]
    fields = coef_ref.shape[0]
    field_ref[...] = jnp.zeros_like(field_ref)
    for d, part in enumerate(parts):

        def one(q, carry, d=d, part=part):
            scatter_row(ranks_ref, d * rows + q, part[q], field_ref, columns)
            return carry

        lax.fori_loop(0, rows, one, 0, unroll=4)
    flat = field_ref.reshape(slots * SUB, LANES)
    first_ref[slots:] = jnp.zeros_like(first_ref[slots:])
    last_ref[slots:] = jnp.zeros_like(last_ref[slots:])
    first_ref[0:slots] = take_column(flat, 0, slots)
    last_ref[0:slots] = take_column(flat, columns - 1, slots)
    flat = coef_ref.reshape(fields * SUB, LANES)
    for j in range(2):
        at = slots + j * fields
        first_ref[at : at + fields] = take_column(flat, j, fields)
        last_ref[at : at + fields] = take_column(flat, columns - 2 + j, fields)


def start_kernel(n, columns, edges, ranks_ref, x_ref, before_ref, after_ref, own_ref, *refs):
    packed, (coef_ref, u_ref, y_ref, diff_ref) = refs[:n], refs[n:]
    slots, fields = x_ref.shape[0], own_ref.shape[0]
    coef_ref[...] = own_ref[...]
    flat = coef_ref.reshape(fields * SUB, LANES)
    for j in range(2):
        at = slots + j * fields
        flat[pl.ds(SUB - 2 + j, fields, stride=SUB), :] = before_ref[at : at + fields]
        flat[pl.ds(columns + j, fields, stride=SUB), :] = after_ref[at : at + fields]
    u_ref[...] = x_ref[...]
    flat = u_ref.reshape(slots * SUB, LANES)
    flat[pl.ds(SUB - 1, slots, stride=SUB), :] = before_ref[0:slots]
    flat[pl.ds(columns, slots, stride=SUB), :] = after_ref[0:slots]
    y_ref[len(edges) :] = jnp.zeros((slots - len(edges), SUB, LANES), jnp.float32)

    def store(s, value):
        y_ref[s] = value

    apply_operator(u_ref, coef_ref, edges, store, diff_ref)
    pack_rows(ranks_ref, packed, y_ref, columns, packed[0].shape[0])


def residual_kernel(n, columns, ranks_ref, *refs):
    forcing, image = refs[:n], refs[n : 2 * n]
    field_ref, first_ref, last_ref = refs[2 * n :]
    rows = forcing[0].shape[0]
    slots = field_ref.shape[0]
    field_ref[...] = jnp.zeros_like(field_ref)
    for d in range(n):

        def one(q, carry, d=d):
            scatter_row(ranks_ref, d * rows + q, forcing[d][q] - image[d][q], field_ref, columns)
            return carry

        lax.fori_loop(0, rows, one, 0, unroll=4)
    flat = field_ref.reshape(slots * SUB, LANES)
    for j in range(2):
        first_ref[j] = take_column(flat, j, slots)
        last_ref[j] = take_column(flat, columns - 2 + j, slots)


def krylov_kernel(
    n, columns, edges, ranks_ref, place_ref, v_ref, before_ref, after_ref, coef_ref, inside_ref, *refs
):
    packed, (table_ref, v0_ref, v1_ref, v2_ref, diff_ref) = refs[:n], refs[n:]
    rows = packed[0].shape[0] // 2
    slots, terms = v_ref.shape[0], len(edges)
    v0_ref[...] = v_ref[...]
    flat = v0_ref.reshape(slots * SUB, LANES)
    for j in range(2):
        flat[pl.ds(SUB - 2 + j, slots, stride=SUB), :] = before_ref[j]
        flat[pl.ds(columns + j, slots, stride=SUB), :] = after_ref[j]
    inside = inside_ref[...] > 0.0

    def store_first(s, value):
        v1_ref[s] = jnp.where(inside, value, 0.0)

    def store_second(s, value):
        v2_ref[s] = value

    for source, target, store in ((v0_ref, v1_ref, store_first), (v1_ref, v2_ref, store_second)):
        target[terms:] = jnp.zeros((slots - terms, SUB, LANES), jnp.float32)
        apply_operator(source, coef_ref, edges, store, diff_ref)
    pack_rows(ranks_ref, packed, v1_ref, columns, rows)
    pack_rows(ranks_ref, packed, v2_ref, columns, rows, rows)
    dot_products(place_ref, columns, v0_ref, v1_ref, v2_ref, table_ref)


def own_sums(count, terms, columns, of_term):
    def one(s, totals):
        return tuple(t + x for t, x in zip(totals, of_term(s)))

    totals = lax.fori_loop(0, terms, one, (jnp.zeros((SUB, LANES), jnp.float32),) * count, unroll=11)
    own = lax.broadcasted_iota(jnp.int32, (SUB, LANES), 0) < columns
    totals = [jnp.where(own, t, 0.0) for t in totals]
    return [jnp.sum(jnp.sum(t, axis=0, keepdims=True), axis=1, keepdims=True) for t in totals]


def dot_products(place_ref, columns, v0_ref, v1_ref, v2_ref, table_ref):
    slots = v0_ref.shape[0]
    aa, ab = own_sums(2, slots, columns, lambda s: (v0_ref[s] * v0_ref[s], v0_ref[s] * v1_ref[s]))
    m = jnp.where(aa > 0.0, ab / jnp.where(aa > 0.0, aa, 1.0), 0.0)

    def products(s):
        a, b, c = v0_ref[s], v1_ref[s], v2_ref[s]
        w = b - m * a
        e = c - m * b
        return a * w, w * w, a * e, w * b, w * e

    entries = [aa, ab, m] + own_sums(5, slots, columns, products)
    lane = lax.broadcasted_iota(jnp.int32, table_ref.shape, 1)
    row = lax.broadcasted_iota(jnp.int32, table_ref.shape, 0)
    table = jnp.zeros(table_ref.shape, jnp.float32)
    for k, value in enumerate(entries):
        table = jnp.where(lane == k, value, table)
    table_ref[...] = jnp.where(row == place_ref[0], table, 0.0)


def step_lengths(table):
    lane = lax.broadcasted_iota(jnp.int32, table.shape, 1)
    aa, ab, m, aw, ww, ae, wb, we = (
        jnp.sum(jnp.where(lane == k, table, 0.0), axis=1, keepdims=True) for k in range(8)
    )

    def total(x):
        return jnp.sum(x, axis=0, keepdims=True)

    norm, curve = total(aa), total(ab)
    step = norm / curve
    g = 1.0 - step * m
    rr = total(g * g * aa - 2.0 * g * step * aw + step * step * ww)
    r_ar = total(g * g * ab - g * step * (ae + wb) + step * step * we)
    mixed = total(2.0 * g * ab - step * (wb + ae))
    beta = rr / norm
    return step, beta, rr / (r_ar + beta * mixed + beta * beta * curve)


def finish_kernel(n, columns, offsets_ref, x_ref, f_ref, *refs):
    tables, image, krylov = refs[:n], refs[n : 2 * n], refs[2 * n : 3 * n]
    approx_ref, residual_ref = refs[3 * n :]
    per = SUB // columns
    rows = image[0].shape[0]
    step, beta, last = step_lengths(functools.reduce(jnp.add, [t[...] for t in tables]))
    whole = step + last * beta
    for d in range(n):
        at = pl.ds(pl.multiple_of(offsets_ref[d], columns), columns)

        def one(q, carry, d=d, at=at):
            y, b, c = image[d][q], krylov[d][q], krylov[d][rows + q]
            for g in range(per):
                part = slice(g * columns, (g + 1) * columns)
                s = q * per + g
                yg, bg, cg = y[part], b[part], c[part]
                v0 = f_ref[s, at] - yg
                r1 = v0 - step * bg
                approx_ref[s, at] = x_ref[s, at] + whole * v0 + last * r1
                residual_ref[s, at] = r1 - last * ((1.0 + beta) * bg - step * cg)
            return carry

        lax.fori_loop(0, rows, one, 0, unroll=2)


class Anywhere:
    def __init__(self, value):
        self.value = value


def call(kernel, scalars, arrays, outs, scratch=()):
    whole = pl.BlockSpec(memory_space=pltpu.VMEM)
    specs = [
        pl.BlockSpec(memory_space=pl.ANY) if isinstance(a, Anywhere) else whole for a in arrays
    ]
    arrays = [a.value if isinstance(a, Anywhere) else a for a in arrays]
    return pl.pallas_call(
        kernel,
        in_specs=[pl.BlockSpec(memory_space=pltpu.SMEM)] * len(scalars) + specs,
        out_specs=[whole] * len(outs),
        out_shape=[jax.ShapeDtypeStruct(s, jnp.float32) for s in outs],
        scratch_shapes=[pltpu.VMEM(s, jnp.float32) for s in scratch],
        compiler_params=PARAMS,
    )(*scalars, *arrays)


def butterfly(value, axis):
    count = lax.axis_size(axis)
    bit = 1
    while bit < count:
        value = value + lax.ppermute(value, axis, [(i, i ^ bit) for i in range(count)])
        bit *= 2
    return value


def per_device(forcing, start_guess, mean_field, mode_fields, multi_index, coupled_slot):
    spaces, n = lax.axis_size("space"), lax.axis_size("chaos")
    i, z = lax.axis_index("space"), lax.axis_index("chaos")
    here, width, lanes = forcing.shape
    modes = mode_fields.shape[0]
    columns = width // n
    rows = here * columns // SUB
    slots = n * here
    edges = term_list(modes)

    def chunk(space, chaos):
        return jnp.where(space % 2 == 0, chaos, n - 1 - chaos)

    def device_at(p):
        tile, c = divmod(p, n)
        return tile * n + (c if tile % 2 == 0 else n - 1 - c)

    line = [(device_at(p), device_at(p + 1)) for p in range(spaces * n - 1)]
    back_line = [(b, a) for a, b in line]
    both = ("space", "chaos")

    def outward(d):
        return [(j, (j + d) % n) for j in range(n)]

    def homeward(d):
        return [(j, (j - d) % n) for j in range(n)]

    offsets = [columns * chunk(i, (z + d) % n) for d in range(n)]

    def sent(parts, way, after=None):
        out = [parts[0]]
        for d in range(1, n):
            value = parts[d]
            if after is not None and after[d] is not None:
                value = lax.optimization_barrier((value, after[d]))[0]
            out.append(lax.ppermute(value, "chaos", way(d)))
        return out

    field, part, fields = (slots, SUB, lanes), (rows, SUB, lanes), (modes + 1, SUB, lanes)
    diff = (3,) + field
    edge = (-(-(slots + 2 * (modes + 1)) // SUB) * SUB, lanes)
    offsets_array = jnp.stack(offsets).astype(jnp.int32)

    cut = functools.partial(cut_kernel, n, columns, rows)
    x_parts = call(cut, [offsets_array], [start_guess, multi_index], [(rows + 1, SUB, lanes)] * n)
    x_parts = sent(list(x_parts), outward)
    ranks = jnp.concatenate([p[rows, 0, :here] for p in x_parts]).astype(jnp.int32)
    f_parts = sent(list(call(cut, [offsets_array], [forcing], [part] * n)), outward)

    stacked = jnp.concatenate([mean_field[None], mode_fields], axis=0)
    own_coef = lax.dynamic_slice_in_dim(stacked, offsets[0], columns, axis=1)
    own_coef = jnp.pad(own_coef, ((0, 0), (0, SUB - columns), (0, 0)))
    sub = lax.broadcasted_iota(jnp.int32, (SUB, lanes), 0)
    position = i * n + chunk(i, z)
    outside = ((position == 0) & (sub >= SUB - 2)) | (
        (position == spaces * n - 1) & (sub >= columns) & (sub < columns + 2)
    )
    inside = jnp.where(outside, 0.0, 1.0)

    x, x_first, x_last = call(
        functools.partial(enter_kernel, n, columns, rows),
        [ranks],
        [own_coef, Anywhere(f_parts[1])] + x_parts,
        [field, edge, edge],
    )
    x_before = lax.ppermute(x_last, both, line)
    x_after = lax.ppermute(x_first, both, back_line)
    *image, coef = call(
        functools.partial(start_kernel, n, columns, edges),
        [ranks],
        [x, x_before, x_after, own_coef],
        [part] * n + [fields],
        [field, field, diff],
    )
    v0, v0_first, v0_last = call(
        functools.partial(residual_kernel, n, columns),
        [ranks],
        f_parts + image,
        [field, (2, slots, lanes), (2, slots, lanes)],
    )
    v0_before = lax.ppermute(v0_last, both, line)
    v0_after = lax.ppermute(v0_first, both, back_line)
    image_home = sent(image, homeward)
    *krylov, table = call(
        functools.partial(krylov_kernel, n, columns, edges),
        [ranks, (i * n + z).astype(jnp.int32)[None]],
        [v0, v0_before, v0_after, coef, inside],
        [(2 * rows, SUB, lanes)] * n + [(-(-spaces * n // SUB) * SUB, lanes)],
        [field, field, field, diff],
    )
    krylov, image_home = lax.optimization_barrier((krylov, image_home))
    krylov_home = sent(krylov, homeward)
    table = butterfly(table, "space")
    tables = sent([table] * n, homeward, [None, krylov_home[n - 1]] + [None] * (n - 2))
    return call(
        functools.partial(finish_kernel, n, columns),
        [offsets_array],
        [start_guess, forcing] + tables + image_home + krylov_home,
        [forcing.shape] * 2,
    )


def solution(mesh):
    placed = (
        P("chaos", "space", None),
        P("chaos", "space", None),
        P("space", None),
        P(None, "space", None),
        P("chaos", None),
        P("chaos", None),
    )
    return jax.shard_map(
        lambda *a: tuple(per_device(*a)),
        mesh=mesh,
        in_specs=placed,
        out_specs=(P("chaos", "space", None), P("chaos", "space", None)),
        check_vma=False,
    )
```

```python
import functools
import math

import jax
import jax.numpy as jnp
import numpy as np
from jax import lax
from jax.experimental import pallas as pl
from jax.experimental.pallas import tpu as pltpu
from jax.sharding import PartitionSpec as P

DEGREE = 3
SUB = 8
LANES = 128
UNROLL = 12
PARAMS = pltpu.CompilerParams(vmem_limit_bytes=12 * 1024 * 1024)


def term_list(modes):
    triples = [
        (a, b, c) for a in range(modes + 1) for b in range(a + 1) for c in range(b + 1)
    ]
    place = {t: i for i, t in enumerate(triples)}
    edges = []
    for t in triples:
        used = [x for x in t if x]
        mine = []
        for k in range(1, modes + 1):
            power = used.count(k)
            if len(used) < DEGREE:
                up = tuple(sorted(used + [k], reverse=True))
                mine.append((place[up + (0,) * (DEGREE - len(up))], k - 1, power + 1))
            if power:
                left = list(used)
                left.remove(k)
                mine.append((place[tuple(left) + (0,) * (DEGREE - len(left))], k - 1, power))
        edges.append(mine)
    return edges


def rank_row(powers):
    modes, here = powers.shape
    above = jnp.zeros((1, here), jnp.int32)
    symbols = [jnp.zeros((1, here), jnp.int32)] * DEGREE
    for k in reversed(range(modes)):
        above += jnp.maximum(powers[k : k + 1], 0)
        symbols = [a + jnp.where(above > n, 1, 0) for n, a in enumerate(symbols)]
    a, b, c = symbols
    rank = a * (a + 1) * (a + 2) // 6 + b * (b + 1) // 2 + c
    return jnp.where(powers[0:1] < 0, math.comb(modes + DEGREE, DEGREE), rank).astype(jnp.float32)


def cut_kernel(n, columns, rows, offsets_ref, source_ref, *refs):
    per = SUB // columns
    index, parts = refs[:-n], refs[-n:]
    for d, out in enumerate(parts):
        at = pl.ds(pl.multiple_of(offsets_ref[d], columns), columns)
        for g in range(per):
            for q in range(rows):
                out[q, g * columns : (g + 1) * columns] = source_ref[q * per + g, at]
    if index:
        ranks = rank_row(index[0][...])
        for out in parts:
            out[rows] = jnp.zeros((SUB, LANES), jnp.float32)
            out[rows, 0:1, 0 : ranks.shape[1]] = ranks


def lane_next(u):
    lane = lax.broadcasted_iota(jnp.int32, u.shape, u.ndim - 1)
    return jnp.where(lane == LANES - 1, 0.0, pltpu.roll(u, LANES - 1, u.ndim - 1))


def lane_before(u):
    lane = lax.broadcasted_iota(jnp.int32, u.shape, u.ndim - 1)
    return jnp.where(lane == 0, 0.0, pltpu.roll(u, 1, u.ndim - 1))


def face_coefficients(coef_ref):
    east, right, left = [], [], []
    for k in range(coef_ref.shape[0]):
        c = coef_ref[k]
        east.append(0.5 * (c + pltpu.roll(c, SUB - 1, 0)))
        right.append(0.5 * (c + lane_next(c)))
        left.append(0.5 * (c + lane_before(c)))
    return east, right, left


def apply_operator(u_ref, coef_ref, edges, store, diff_ref):
    terms = len(edges)

    u = u_ref[0:terms]
    diff_ref[0, 0:terms] = pltpu.roll(u, SUB - 1, 1) - u
    diff_ref[1, 0:terms] = u - lane_next(u)
    diff_ref[2, 0:terms] = u - lane_before(u)
    east, right, left = face_coefficients(coef_ref)
    for s in range(terms):
        groups = {1: [(s, 0)]}
        for t, k, weight in edges[s]:
            groups.setdefault(weight, []).append((t, k + 1))
        across = along = None
        for weight, members in groups.items():
            e = a = None
            for t, k in members:
                de = east[k] * diff_ref[0, t]
                da = right[k] * diff_ref[1, t] + left[k] * diff_ref[2, t]
                e = de if e is None else e + de
                a = da if a is None else a + da
            if weight > 1:
                e, a = e * math.sqrt(weight), a * math.sqrt(weight)
            across = e if across is None else across + e
            along = a if along is None else along + a
        store(s, pltpu.roll(across, 1, 0) - across + along)


def pack_rows(ranks_ref, packed_refs, field_ref, columns, rows, first=0):
    per = SUB // columns
    sub = lax.broadcasted_iota(jnp.int32, (SUB, LANES), 0)
    for d, out in enumerate(packed_refs):

        def one(q, carry, d=d, out=out):
            row = field_ref[ranks_ref[(d * rows + q) * per]]
            for g in range(1, per):
                other = field_ref[ranks_ref[(d * rows + q) * per + g]]
                row = jnp.where(sub < g * columns, row, pltpu.roll(other, g * columns, 0))
            out[first + q] = row
            return carry

        lax.fori_loop(0, rows, one, 0, unroll=min(rows, UNROLL))


def scatter_row(ranks_ref, at, row, field_ref, columns):
    per = SUB // columns
    for g in range(per):
        part = row if g == 0 else pltpu.roll(row, SUB - g * columns, 0)
        field_ref[ranks_ref[at * per + g], 0:columns] = part[0:columns]


def take_column(flat_ref, j, rows):
    return flat_ref[pl.ds(j, rows, stride=SUB), :]


def enter_kernel(n, columns, rows, ranks_ref, coef_ref, *refs):
    parts, (field_ref, first_ref, last_ref) = refs[:n], refs[n:]
    slots = field_ref.shape[0]
    fields = coef_ref.shape[0]
    field_ref[...] = jnp.zeros_like(field_ref)
    for d, part in enumerate(parts):

        def one(q, carry, d=d, part=part):
            scatter_row(ranks_ref, d * rows + q, part[q], field_ref, columns)
            return carry

        lax.fori_loop(0, rows, one, 0, unroll=min(rows, UNROLL))
    flat = field_ref.reshape(slots * SUB, LANES)
    terms = first_ref.shape[0] - 2 * fields
    first_ref[0:terms] = take_column(flat, 0, terms)
    last_ref[0:terms] = take_column(flat, columns - 1, terms)
    flat = coef_ref.reshape(fields * SUB, LANES)
    for j in range(2):
        at = terms + j * fields
        first_ref[at : at + fields] = take_column(flat, j, fields)
        last_ref[at : at + fields] = take_column(flat, columns - 2 + j, fields)


def start_kernel(columns, edges, x_ref, before_ref, after_ref, own_ref, y_ref, coef_ref, u_ref, diff_ref):
    slots, fields, terms = x_ref.shape[0], own_ref.shape[0], len(edges)
    coef_ref[...] = own_ref[...]
    flat = coef_ref.reshape(fields * SUB, LANES)
    for j in range(2):
        at = terms + j * fields
        flat[pl.ds(SUB - 2 + j, fields, stride=SUB), :] = before_ref[at : at + fields]
        flat[pl.ds(columns + j, fields, stride=SUB), :] = after_ref[at : at + fields]
    u_ref[...] = x_ref[...]
    flat = u_ref.reshape(slots * SUB, LANES)
    flat[pl.ds(SUB - 1, terms, stride=SUB), :] = before_ref[0:terms]
    flat[pl.ds(columns, terms, stride=SUB), :] = after_ref[0:terms]
    y_ref[len(edges) :] = jnp.zeros((slots - len(edges), SUB, LANES), jnp.float32)

    def store(s, value):
        y_ref[s] = value

    apply_operator(u_ref, coef_ref, edges, store, diff_ref)


def residual_kernel(n, columns, rows, ranks_ref, y_ref, *refs):
    forcing, packed, (field_ref, first_ref, last_ref) = refs[:n], refs[n : 2 * n], refs[2 * n :]
    per = SUB // columns
    slots = field_ref.shape[0]
    sub = lax.broadcasted_iota(jnp.int32, (SUB, LANES), 0)
    field_ref[...] = jnp.zeros_like(field_ref)
    for d in range(n):

        def one(q, carry, d=d):
            at = [ranks_ref[(d * rows + q) * per + g] for g in range(per)]
            y = y_ref[at[0]]
            for g in range(1, per):
                y = jnp.where(sub < g * columns, y, pltpu.roll(y_ref[at[g]], g * columns, 0))
            v = forcing[d][q] - y
            packed[d][q] = v
            for g in range(per):
                own = v if g == 0 else pltpu.roll(v, SUB - g * columns, 0)
                field_ref[at[g], 0:columns] = own[0:columns]
            return carry

        lax.fori_loop(0, rows, one, 0, unroll=min(rows, UNROLL))
    flat = field_ref.reshape(slots * SUB, LANES)
    for j in range(2):
        first_ref[j] = take_column(flat, j, slots)
        last_ref[j] = take_column(flat, columns - 2 + j, slots)


def krylov_kernel(
    n, columns, edges, ranks_ref, place_ref, v_ref, before_ref, after_ref, coef_ref, inside_ref, *refs
):
    packed, (table_ref, v0_ref, v1_ref, v2_ref, diff_ref) = refs[:n], refs[n:]
    rows = packed[0].shape[0] // 2
    slots, terms = v_ref.shape[0], len(edges)
    v0_ref[...] = v_ref[...]
    flat = v0_ref.reshape(slots * SUB, LANES)
    for j in range(2):
        flat[pl.ds(SUB - 2 + j, slots, stride=SUB), :] = before_ref[j]
        flat[pl.ds(columns + j, slots, stride=SUB), :] = after_ref[j]
    inside = inside_ref[...] > 0.0

    def store_first(s, value):
        v1_ref[s] = jnp.where(inside, value, 0.0)

    def store_second(s, value):
        v2_ref[s] = value

    for source, target, store in ((v0_ref, v1_ref, store_first), (v1_ref, v2_ref, store_second)):
        target[terms:] = jnp.zeros((slots - terms, SUB, LANES), jnp.float32)
        apply_operator(source, coef_ref, edges, store, diff_ref)
    pack_rows(ranks_ref, packed, v1_ref, columns, rows)
    pack_rows(ranks_ref, packed, v2_ref, columns, rows, rows)
    dot_products(place_ref, columns, v0_ref, v1_ref, v2_ref, table_ref)


def own_sums(count, terms, columns, of_term):
    def one(s, totals):
        return tuple(t + x for t, x in zip(totals, of_term(s)))

    totals = lax.fori_loop(0, terms, one, (jnp.zeros((SUB, LANES), jnp.float32),) * count, unroll=16)
    own = lax.broadcasted_iota(jnp.int32, (SUB, LANES), 0) < columns
    totals = [jnp.where(own, t, 0.0) for t in totals]
    return [jnp.sum(jnp.sum(t, axis=0, keepdims=True), axis=1, keepdims=True) for t in totals]


def dot_products(place_ref, columns, v0_ref, v1_ref, v2_ref, table_ref):
    slots = v0_ref.shape[0]
    aa, ab = own_sums(2, slots, columns, lambda s: (v0_ref[s] * v0_ref[s], v0_ref[s] * v1_ref[s]))
    m = jnp.where(aa > 0.0, ab / jnp.where(aa > 0.0, aa, 1.0), 0.0)

    def products(s):
        a, b, c = v0_ref[s], v1_ref[s], v2_ref[s]
        w = b - m * a
        e = c - m * b
        return a * w, w * w, a * e, w * b, w * e

    entries = [aa, ab, m] + own_sums(5, slots, columns, products)
    lane = lax.broadcasted_iota(jnp.int32, table_ref.shape, 1)
    row = lax.broadcasted_iota(jnp.int32, table_ref.shape, 0)
    table = jnp.zeros(table_ref.shape, jnp.float32)
    for k, value in enumerate(entries):
        table = jnp.where(lane == k, value, table)
    table_ref[...] = jnp.where(row == place_ref[0], table, 0.0)


def step_lengths(table):
    lane = lax.broadcasted_iota(jnp.int32, table.shape, 1)
    aa, ab, m, aw, ww, ae, wb, we = (
        jnp.sum(jnp.where(lane == k, table, 0.0), axis=1, keepdims=True) for k in range(8)
    )

    def total(x):
        return jnp.sum(x, axis=0, keepdims=True)

    norm, curve = total(aa), total(ab)
    step = norm / curve
    g = 1.0 - step * m
    rr = total(g * g * aa - 2.0 * g * step * aw + step * step * ww)
    r_ar = total(g * g * ab - g * step * (ae + wb) + step * step * we)
    mixed = total(2.0 * g * ab - step * (wb + ae))
    beta = rr / norm
    return step, beta, rr / (r_ar + beta * mixed + beta * beta * curve)


def finish_kernel(n, columns, offsets_ref, x_ref, *refs):
    tables, v0, krylov = refs[:n], refs[n : 2 * n], refs[2 * n : 3 * n]
    approx_ref, residual_ref = refs[3 * n :]
    per = SUB // columns
    rows = v0[0].shape[0]
    step, beta, last = step_lengths(functools.reduce(jnp.add, [t[...] for t in tables]))
    whole = step + last * beta
    for d in range(n):
        at = pl.ds(pl.multiple_of(offsets_ref[d], columns), columns)

        def one(q, carry, d=d, at=at):
            a, b, c = v0[d][q], krylov[d][q], krylov[d][rows + q]
            for g in range(per):
                part = slice(g * columns, (g + 1) * columns)
                s = q * per + g
                ag, bg, cg = a[part], b[part], c[part]
                r1 = ag - step * bg
                approx_ref[s, at] = x_ref[s, at] + whole * ag + last * r1
                residual_ref[s, at] = r1 - last * ((1.0 + beta) * bg - step * cg)
            return carry

        lax.fori_loop(0, rows, one, 0, unroll=min(rows, UNROLL))


class Anywhere:
    def __init__(self, value):
        self.value = value


def call(kernel, scalars, arrays, outs, scratch=()):
    whole = pl.BlockSpec(memory_space=pltpu.VMEM)
    specs = [
        pl.BlockSpec(memory_space=pl.ANY) if isinstance(a, Anywhere) else whole for a in arrays
    ]
    arrays = [a.value if isinstance(a, Anywhere) else a for a in arrays]
    return pl.pallas_call(
        kernel,
        in_specs=[pl.BlockSpec(memory_space=pltpu.SMEM)] * len(scalars) + specs,
        out_specs=[whole] * len(outs),
        out_shape=[jax.ShapeDtypeStruct(s, jnp.float32) for s in outs],
        scratch_shapes=[pltpu.VMEM(s, jnp.float32) for s in scratch],
        compiler_params=PARAMS,
    )(*scalars, *arrays)


def butterfly(value, axis):
    count = lax.axis_size(axis)
    bit = 1
    while bit < count:
        value = value + lax.ppermute(value, axis, [(i, i ^ bit) for i in range(count)])
        bit *= 2
    return value


def per_device(forcing, start_guess, mean_field, mode_fields, multi_index, coupled_slot):
    spaces, n = lax.axis_size("space"), lax.axis_size("chaos")
    i, z = lax.axis_index("space"), lax.axis_index("chaos")
    here, width, lanes = forcing.shape
    modes = mode_fields.shape[0]
    columns = width // n
    rows = here * columns // SUB
    slots = n * here
    edges = term_list(modes)

    def chunk(space, chaos):
        return jnp.where(space % 2 == 0, chaos, n - 1 - chaos)

    def device_at(p):
        tile, c = divmod(p, n)
        return tile * n + (c if tile % 2 == 0 else n - 1 - c)

    line = [(device_at(p), device_at(p + 1)) for p in range(spaces * n - 1)]
    back_line = [(b, a) for a, b in line]
    both = ("space", "chaos")

    def outward(d):
        return [(j, (j + d) % n) for j in range(n)]

    def homeward(d):
        return [(j, (j - d) % n) for j in range(n)]

    offsets = [columns * chunk(i, (z + d) % n) for d in range(n)]

    def sent(parts, way, after=None):
        out = [parts[0]]
        for d in range(1, n):
            value = parts[d]
            if after is not None and after[d] is not None:
                value = lax.optimization_barrier((value, after[d]))[0]
            out.append(lax.ppermute(value, "chaos", way(d)))
        return out

    field, part, fields = (slots, SUB, lanes), (rows, SUB, lanes), (modes + 1, SUB, lanes)
    diff = (3,) + field
    edge = (len(edges) + 2 * (modes + 1), lanes)
    offsets_array = jnp.stack(offsets).astype(jnp.int32)

    f_rows = max(rows, edge[0] // SUB + 1)
    f_shapes = [(f_rows + (d != n // 2), SUB, lanes) for d in range(n)]
    cut = functools.partial(cut_kernel, n, columns, rows)
    x_parts = call(cut, [offsets_array], [start_guess, multi_index.T], [(rows + 1 + (d == n // 2), SUB, lanes) for d in range(n)])
    x_parts = sent(list(x_parts), outward)
    ranks = jnp.concatenate([p[rows, 0, :here] for p in x_parts]).astype(jnp.int32)
    f_parts = sent(list(call(cut, [offsets_array], [forcing], f_shapes)), outward)

    stacked = jnp.concatenate([mean_field[None], mode_fields], axis=0)
    own_coef = lax.dynamic_slice_in_dim(stacked, offsets[0], columns, axis=1)
    own_coef = jnp.pad(own_coef, ((0, 0), (0, SUB - columns), (0, 0)))
    sub = lax.broadcasted_iota(jnp.int32, (SUB, lanes), 0)
    position = i * n + chunk(i, z)
    outside = ((position == 0) & (sub >= SUB - 2)) | (
        (position == spaces * n - 1) & (sub >= columns) & (sub < columns + 2)
    )
    inside = jnp.where(outside, 0.0, 1.0)

    x, x_first, x_last = call(
        functools.partial(enter_kernel, n, columns, rows),
        [ranks],
        [own_coef] + x_parts,
        [field, edge, edge],
    )
    x_before = lax.ppermute(x_last, both, line)
    x_after = lax.ppermute(x_first, both, back_line)
    image, coef = call(
        functools.partial(start_kernel, columns, edges),
        [],
        [x, x_before, x_after, own_coef],
        [field, fields],
        [field, diff],
    )
    *v0_parts, v0, v0_first, v0_last = call(
        functools.partial(residual_kernel, n, columns, rows),
        [ranks],
        [image] + f_parts,
        [part] * n + [field, (2, slots, lanes), (2, slots, lanes)],
    )
    v0_before = lax.ppermute(v0_last, both, line)
    v0_after = lax.ppermute(v0_first, both, back_line)
    v0_home = sent(v0_parts, homeward)
    *krylov, table = call(
        functools.partial(krylov_kernel, n, columns, edges),
        [ranks, (i * n + z).astype(jnp.int32)[None]],
        [v0, v0_before, v0_after, coef, inside],
        [(2 * rows, SUB, lanes)] * n + [(-(-spaces * n // SUB) * SUB, lanes)],
        [field, field, field, diff],
    )
    krylov, v0_home = lax.optimization_barrier((krylov, v0_home))
    krylov_home = sent(krylov, homeward)
    table = butterfly(table, "space")
    tables = sent([table] * n, homeward, [None, krylov_home[n - 1]] + [None] * (n - 2))
    return call(
        functools.partial(finish_kernel, n, columns),
        [offsets_array],
        [start_guess] + tables + v0_home + krylov_home,
        [forcing.shape] * 2,
    )


def solution(mesh):
    placed = (
        P("chaos", "space", None),
        P("chaos", "space", None),
        P("space", None),
        P(None, "space", None),
        P("chaos", None),
        P("chaos", None),
    )
    return jax.shard_map(
        lambda *a: tuple(per_device(*a)),
        mesh=mesh,
        in_specs=placed,
        out_specs=(P("chaos", "space", None), P("chaos", "space", None)),
        check_vma=False,
    )
```

```python
import functools
import math

import jax
import jax.numpy as jnp
import numpy as np
from jax import lax
from jax.experimental import pallas as pl
from jax.experimental.pallas import tpu as pltpu
from jax.sharding import PartitionSpec as P

DEGREE = 3
SUB = 8
LANES = 128
UNROLL = 12
SPARE_ROWS = 3
PARAMS = pltpu.CompilerParams(vmem_limit_bytes=12 * 1024 * 1024)


def term_list(modes):
    triples = [
        (a, b, c) for a in range(modes + 1) for b in range(a + 1) for c in range(b + 1)
    ]
    place = {t: i for i, t in enumerate(triples)}
    edges = []
    for t in triples:
        used = [x for x in t if x]
        mine = []
        for k in range(1, modes + 1):
            power = used.count(k)
            if len(used) < DEGREE:
                up = tuple(sorted(used + [k], reverse=True))
                mine.append((place[up + (0,) * (DEGREE - len(up))], k - 1, power + 1))
            if power:
                left = list(used)
                left.remove(k)
                mine.append((place[tuple(left) + (0,) * (DEGREE - len(left))], k - 1, power))
        edges.append(mine)
    return edges


def rank_row(powers):
    modes, here = powers.shape
    above = jnp.zeros((1, here), jnp.int32)
    symbols = [jnp.zeros((1, here), jnp.int32)] * DEGREE
    for k in reversed(range(modes)):
        above += jnp.maximum(powers[k : k + 1], 0)
        symbols = [a + jnp.where(above > n, 1, 0) for n, a in enumerate(symbols)]
    a, b, c = symbols
    rank = a * (a + 1) * (a + 2) // 6 + b * (b + 1) // 2 + c
    return jnp.where(powers[0:1] < 0, math.comb(modes + DEGREE, DEGREE), rank).astype(jnp.float32)


def cut_kernel(n, columns, rows, offsets_ref, source_ref, *refs):
    per = SUB // columns
    index, parts = refs[:-n], refs[-n:]
    for d, out in enumerate(parts):
        at = pl.ds(pl.multiple_of(offsets_ref[d], columns), columns)
        for g in range(per):
            for q in range(rows):
                out[q, g * columns : (g + 1) * columns] = source_ref[q * per + g, at]
    if index:
        ranks = rank_row(index[0][...])
        for out in parts:
            out[rows] = jnp.zeros((SUB, LANES), jnp.float32)
            out[rows, 0:1, 0 : ranks.shape[1]] = ranks


def lane_next(u):
    lane = lax.broadcasted_iota(jnp.int32, u.shape, u.ndim - 1)
    return jnp.where(lane == LANES - 1, 0.0, pltpu.roll(u, LANES - 1, u.ndim - 1))


def lane_before(u):
    lane = lax.broadcasted_iota(jnp.int32, u.shape, u.ndim - 1)
    return jnp.where(lane == 0, 0.0, pltpu.roll(u, 1, u.ndim - 1))


def face_coefficients(coef_ref):
    east, right, left = [], [], []
    for k in range(coef_ref.shape[0]):
        c = coef_ref[k]
        east.append(0.5 * (c + pltpu.roll(c, SUB - 1, 0)))
        right.append(0.5 * (c + lane_next(c)))
        left.append(0.5 * (c + lane_before(c)))
    return east, right, left


def apply_operator(u_ref, coef_ref, edges, store, diff_ref):
    terms = len(edges)

    u = u_ref[0:terms]
    diff_ref[0, 0:terms] = pltpu.roll(u, SUB - 1, 1) - u
    diff_ref[1, 0:terms] = u - lane_next(u)
    diff_ref[2, 0:terms] = u - lane_before(u)
    east, right, left = face_coefficients(coef_ref)
    for s in range(terms):
        groups = {1: [(s, 0)]}
        for t, k, weight in edges[s]:
            groups.setdefault(weight, []).append((t, k + 1))
        across = along = None
        for weight, members in groups.items():
            e = a = None
            for t, k in members:
                de = east[k] * diff_ref[0, t]
                da = right[k] * diff_ref[1, t] + left[k] * diff_ref[2, t]
                e = de if e is None else e + de
                a = da if a is None else a + da
            if weight > 1:
                e, a = e * math.sqrt(weight), a * math.sqrt(weight)
            across = e if across is None else across + e
            along = a if along is None else along + a
        store(s, pltpu.roll(across, 1, 0) - across + along)


def pack_rows(ranks_ref, packed_refs, field_ref, columns, rows, first=0):
    per = SUB // columns
    sub = lax.broadcasted_iota(jnp.int32, (SUB, LANES), 0)
    for d, out in enumerate(packed_refs):

        def one(q, carry, d=d, out=out):
            row = field_ref[ranks_ref[(d * rows + q) * per]]
            for g in range(1, per):
                other = field_ref[ranks_ref[(d * rows + q) * per + g]]
                row = jnp.where(sub < g * columns, row, pltpu.roll(other, g * columns, 0))
            out[first + q] = row
            return carry

        lax.fori_loop(0, rows, one, 0, unroll=min(rows, UNROLL))


def scatter_row(ranks_ref, at, row, field_ref, columns):
    per = SUB // columns
    for g in range(per):
        part = row if g == 0 else pltpu.roll(row, SUB - g * columns, 0)
        field_ref[ranks_ref[at * per + g], 0:columns] = part[0:columns]


def take_column(flat_ref, j, rows):
    return flat_ref[pl.ds(j, rows, stride=SUB), :]


def enter_kernel(n, columns, rows, ranks_ref, coef_ref, *refs):
    parts, (field_ref, first_ref, last_ref) = refs[:n], refs[n:]
    slots = field_ref.shape[0]
    fields = coef_ref.shape[0]
    field_ref[...] = jnp.zeros_like(field_ref)
    for d, part in enumerate(parts):

        def one(q, carry, d=d, part=part):
            scatter_row(ranks_ref, d * rows + q, part[q], field_ref, columns)
            return carry

        lax.fori_loop(0, rows, one, 0, unroll=min(rows, UNROLL))
    flat = field_ref.reshape(slots * SUB, LANES)
    terms = first_ref.shape[0] - 2 * fields
    first_ref[0:terms] = take_column(flat, 0, terms)
    last_ref[0:terms] = take_column(flat, columns - 1, terms)
    flat = coef_ref.reshape(fields * SUB, LANES)
    for j in range(2):
        at = terms + j * fields
        first_ref[at : at + fields] = take_column(flat, j, fields)
        last_ref[at : at + fields] = take_column(flat, columns - 2 + j, fields)


def start_kernel(columns, edges, x_ref, before_ref, after_ref, own_ref, y_ref, coef_ref, u_ref, diff_ref):
    slots, fields, terms = x_ref.shape[0], own_ref.shape[0], len(edges)
    coef_ref[...] = own_ref[...]
    flat = coef_ref.reshape(fields * SUB, LANES)
    for j in range(2):
        at = terms + j * fields
        flat[pl.ds(SUB - 2 + j, fields, stride=SUB), :] = before_ref[at : at + fields]
        flat[pl.ds(columns + j, fields, stride=SUB), :] = after_ref[at : at + fields]
    u_ref[...] = x_ref[...]
    flat = u_ref.reshape(slots * SUB, LANES)
    flat[pl.ds(SUB - 1, terms, stride=SUB), :] = before_ref[0:terms]
    flat[pl.ds(columns, terms, stride=SUB), :] = after_ref[0:terms]
    y_ref[len(edges) :] = jnp.zeros((slots - len(edges), SUB, LANES), jnp.float32)

    def store(s, value):
        y_ref[s] = value

    apply_operator(u_ref, coef_ref, edges, store, diff_ref)


def residual_kernel(n, columns, rows, ranks_ref, y_ref, *refs):
    forcing, packed, (field_ref, first_ref, last_ref) = refs[:n], refs[n : 2 * n], refs[2 * n :]
    per = SUB // columns
    slots = field_ref.shape[0]
    sub = lax.broadcasted_iota(jnp.int32, (SUB, LANES), 0)
    field_ref[...] = jnp.zeros_like(field_ref)
    for d in range(n):

        def one(q, carry, d=d):
            at = [ranks_ref[(d * rows + q) * per + g] for g in range(per)]
            y = y_ref[at[0]]
            for g in range(1, per):
                y = jnp.where(sub < g * columns, y, pltpu.roll(y_ref[at[g]], g * columns, 0))
            v = forcing[d][q] - y
            packed[d][q] = v
            for g in range(per):
                own = v if g == 0 else pltpu.roll(v, SUB - g * columns, 0)
                field_ref[at[g], 0:columns] = own[0:columns]
            return carry

        lax.fori_loop(0, rows, one, 0, unroll=min(rows, UNROLL))
    flat = field_ref.reshape(slots * SUB, LANES)
    for j in range(2):
        first_ref[j] = take_column(flat, j, slots)
        last_ref[j] = take_column(flat, columns - 2 + j, slots)


def krylov_kernel(
    n, columns, edges, ranks_ref, place_ref, v_ref, before_ref, after_ref, coef_ref, inside_ref, *refs
):
    packed, (table_ref, v0_ref, v1_ref, v2_ref, diff_ref) = refs[:n], refs[n:]
    rows = packed[0].shape[0] // 2
    slots, terms = v_ref.shape[0], len(edges)
    v0_ref[...] = v_ref[...]
    flat = v0_ref.reshape(slots * SUB, LANES)
    for j in range(2):
        flat[pl.ds(SUB - 2 + j, slots, stride=SUB), :] = before_ref[j]
        flat[pl.ds(columns + j, slots, stride=SUB), :] = after_ref[j]
    inside = inside_ref[...] > 0.0

    def store_first(s, value):
        v1_ref[s] = jnp.where(inside, value, 0.0)

    def store_second(s, value):
        v2_ref[s] = value

    for source, target, store in ((v0_ref, v1_ref, store_first), (v1_ref, v2_ref, store_second)):
        target[terms:] = jnp.zeros((slots - terms, SUB, LANES), jnp.float32)
        apply_operator(source, coef_ref, edges, store, diff_ref)
    pack_rows(ranks_ref, packed, v1_ref, columns, rows)
    pack_rows(ranks_ref, packed, v2_ref, columns, rows, rows)
    dot_products(place_ref, columns, v0_ref, v1_ref, v2_ref, table_ref)


def own_sums(count, terms, columns, of_term):
    def one(s, totals):
        return tuple(t + x for t, x in zip(totals, of_term(s)))

    totals = lax.fori_loop(0, terms, one, (jnp.zeros((SUB, LANES), jnp.float32),) * count, unroll=16)
    own = lax.broadcasted_iota(jnp.int32, (SUB, LANES), 0) < columns
    totals = [jnp.where(own, t, 0.0) for t in totals]
    return [jnp.sum(jnp.sum(t, axis=0, keepdims=True), axis=1, keepdims=True) for t in totals]


def dot_products(place_ref, columns, v0_ref, v1_ref, v2_ref, table_ref):
    slots = v0_ref.shape[0]
    aa, ab = own_sums(2, slots, columns, lambda s: (v0_ref[s] * v0_ref[s], v0_ref[s] * v1_ref[s]))
    m = jnp.where(aa > 0.0, ab / jnp.where(aa > 0.0, aa, 1.0), 0.0)

    def products(s):
        a, b, c = v0_ref[s], v1_ref[s], v2_ref[s]
        w = b - m * a
        e = c - m * b
        return a * w, w * w, a * e, w * b, w * e

    entries = [aa, ab, m] + own_sums(5, slots, columns, products)
    lane = lax.broadcasted_iota(jnp.int32, table_ref.shape, 1)
    row = lax.broadcasted_iota(jnp.int32, table_ref.shape, 0)
    table = jnp.zeros(table_ref.shape, jnp.float32)
    for k, value in enumerate(entries):
        table = jnp.where(lane == k, value, table)
    table_ref[...] = jnp.where(row == place_ref[0], table, 0.0)


def step_lengths(table):
    lane = lax.broadcasted_iota(jnp.int32, table.shape, 1)
    aa, ab, m, aw, ww, ae, wb, we = (
        jnp.sum(jnp.where(lane == k, table, 0.0), axis=1, keepdims=True) for k in range(8)
    )

    def total(x):
        return jnp.sum(x, axis=0, keepdims=True)

    norm, curve = total(aa), total(ab)
    step = norm / curve
    g = 1.0 - step * m
    rr = total(g * g * aa - 2.0 * g * step * aw + step * step * ww)
    r_ar = total(g * g * ab - g * step * (ae + wb) + step * step * we)
    mixed = total(2.0 * g * ab - step * (wb + ae))
    beta = rr / norm
    return step, beta, rr / (r_ar + beta * mixed + beta * beta * curve)


def finish_kernel(n, columns, offsets_ref, x_ref, *refs):
    tables, v0, krylov = refs[:n], refs[n : 2 * n], refs[2 * n : 3 * n]
    approx_ref, residual_ref = refs[3 * n :]
    per = SUB // columns
    rows = v0[0].shape[0]
    step, beta, last = step_lengths(functools.reduce(jnp.add, [t[...] for t in tables]))
    whole = step + last * beta
    for d in range(n):
        at = pl.ds(pl.multiple_of(offsets_ref[d], columns), columns)

        def one(q, carry, d=d, at=at):
            a, b, c = v0[d][q], krylov[d][q], krylov[d][rows + q]
            for g in range(per):
                part = slice(g * columns, (g + 1) * columns)
                s = q * per + g
                ag, bg, cg = a[part], b[part], c[part]
                r1 = ag - step * bg
                approx_ref[s, at] = x_ref[s, at] + whole * ag + last * r1
                residual_ref[s, at] = r1 - last * ((1.0 + beta) * bg - step * cg)
            return carry

        lax.fori_loop(0, rows, one, 0, unroll=min(rows, UNROLL))


class Anywhere:
    def __init__(self, value):
        self.value = value


def call(kernel, scalars, arrays, outs, scratch=()):
    whole = pl.BlockSpec(memory_space=pltpu.VMEM)
    specs = [
        pl.BlockSpec(memory_space=pl.ANY) if isinstance(a, Anywhere) else whole for a in arrays
    ]
    arrays = [a.value if isinstance(a, Anywhere) else a for a in arrays]
    return pl.pallas_call(
        kernel,
        in_specs=[pl.BlockSpec(memory_space=pltpu.SMEM)] * len(scalars) + specs,
        out_specs=[whole] * len(outs),
        out_shape=[jax.ShapeDtypeStruct(s, jnp.float32) for s in outs],
        scratch_shapes=[pltpu.VMEM(s, jnp.float32) for s in scratch],
        compiler_params=PARAMS,
    )(*scalars, *arrays)


def butterfly(value, axis):
    count = lax.axis_size(axis)
    bit = 1
    while bit < count:
        value = value + lax.ppermute(value, axis, [(i, i ^ bit) for i in range(count)])
        bit *= 2
    return value


def per_device(forcing, start_guess, mean_field, mode_fields, multi_index, coupled_slot):
    spaces, n = lax.axis_size("space"), lax.axis_size("chaos")
    i, z = lax.axis_index("space"), lax.axis_index("chaos")
    here, width, lanes = forcing.shape
    modes = mode_fields.shape[0]
    columns = width // n
    rows = here * columns // SUB
    slots = n * here
    edges = term_list(modes)

    def chunk(space, chaos):
        return jnp.where(space % 2 == 0, chaos, n - 1 - chaos)

    def device_at(p):
        tile, c = divmod(p, n)
        return tile * n + (c if tile % 2 == 0 else n - 1 - c)

    line = [(device_at(p), device_at(p + 1)) for p in range(spaces * n - 1)]
    back_line = [(b, a) for a, b in line]
    both = ("space", "chaos")

    def outward(d):
        return [(j, (j + d) % n) for j in range(n)]

    def homeward(d):
        return [(j, (j - d) % n) for j in range(n)]

    offsets = [columns * chunk(i, (z + d) % n) for d in range(n)]

    def longer(count):
        return [(count + (d == n // 2), SUB, lanes) for d in range(n)]

    def sent(parts, way, after=None):
        out = [parts[0]]
        for d in range(1, n):
            value = parts[d]
            if after is not None and after[d] is not None:
                value = lax.optimization_barrier((value, after[d]))[0]
            out.append(lax.ppermute(value, "chaos", way(d)))
        return out

    field, part, fields = (slots, SUB, lanes), (rows, SUB, lanes), (modes + 1, SUB, lanes)
    diff = (3,) + field
    edge = (len(edges) + 2 * (modes + 1), lanes)
    offsets_array = jnp.stack(offsets).astype(jnp.int32)

    f_rows = max(rows, edge[0] // SUB + 1)
    f_shapes = [(f_rows, SUB, lanes)] * n
    cut = functools.partial(cut_kernel, n, columns, rows)
    x_parts = call(cut, [offsets_array], [start_guess, multi_index.T], longer(rows + 1))
    x_parts = sent(list(x_parts), outward)
    ranks = jnp.concatenate([p[rows, 0, :here] for p in x_parts]).astype(jnp.int32)
    f_parts = sent(list(call(cut, [offsets_array], [forcing], f_shapes)), outward)

    stacked = jnp.concatenate([mean_field[None], mode_fields], axis=0)
    own_coef = lax.dynamic_slice_in_dim(stacked, offsets[0], columns, axis=1)
    own_coef = jnp.pad(own_coef, ((0, 0), (0, SUB - columns), (0, 0)))
    sub = lax.broadcasted_iota(jnp.int32, (SUB, lanes), 0)
    position = i * n + chunk(i, z)
    outside = ((position == 0) & (sub >= SUB - 2)) | (
        (position == spaces * n - 1) & (sub >= columns) & (sub < columns + 2)
    )
    inside = jnp.where(outside, 0.0, 1.0)

    x, x_first, x_last = call(
        functools.partial(enter_kernel, n, columns, rows),
        [ranks],
        [own_coef] + x_parts,
        [field, edge, edge],
    )
    x_before = lax.ppermute(x_last, both, line)
    x_after = lax.ppermute(x_first, both, back_line)
    image, coef = call(
        functools.partial(start_kernel, columns, edges),
        [],
        [x, x_before, x_after, own_coef],
        [field, fields],
        [field, diff],
    )
    *v0_parts, v0, v0_first, v0_last = call(
        functools.partial(residual_kernel, n, columns, rows),
        [ranks],
        [image] + f_parts,
        [part] * n + [field, (2, slots, lanes), (2, slots, lanes)],
    )
    v0_before = lax.ppermute(v0_last, both, line)
    v0_after = lax.ppermute(v0_first, both, back_line)
    v0_home = sent(v0_parts, homeward)
    table_rows = -(-spaces * n // SUB) * SUB
    *krylov, table = call(
        functools.partial(krylov_kernel, n, columns, edges),
        [ranks, (i * n + z).astype(jnp.int32)[None]],
        [v0, v0_before, v0_after, coef, inside],
        [(2 * rows, SUB, lanes)] * n + [(SPARE_ROWS + table_rows, lanes)],
        [field, field, field, diff],
    )
    far = n // 2
    near_home = [v0_home[d] for d in range(1, n) if d != far]
    krylov, near_home = lax.optimization_barrier((krylov, near_home))
    krylov_home = sent(krylov, homeward)
    table, v0_home[far] = lax.optimization_barrier((table, v0_home[far]))
    table = butterfly(table, "space")[:table_rows]
    tables = sent([table] * n, homeward, [None, krylov_home[n - 1]] + [None] * (n - 2))
    return call(
        functools.partial(finish_kernel, n, columns),
        [offsets_array],
        [start_guess] + tables + v0_home + krylov_home,
        [forcing.shape] * 2,
    )


def solution(mesh):
    placed = (
        P("chaos", "space", None),
        P("chaos", "space", None),
        P("space", None),
        P(None, "space", None),
        P("chaos", None),
        P("chaos", None),
    )
    return jax.shard_map(
        lambda *a: tuple(per_device(*a)),
        mesh=mesh,
        in_specs=placed,
        out_specs=(P("chaos", "space", None), P("chaos", "space", None)),
        check_vma=False,
    )
```

```python
import functools
import math

import jax
import jax.numpy as jnp
import numpy as np
from jax import lax
from jax.experimental import pallas as pl
from jax.experimental.pallas import tpu as pltpu
from jax.sharding import PartitionSpec as P

DEGREE = 3
SUB = 8
LANES = 128
UNROLL = 12
SPARE_ROWS = 3
PARAMS = pltpu.CompilerParams(vmem_limit_bytes=12 * 1024 * 1024)


def term_list(modes):
    triples = [
        (a, b, c) for a in range(modes + 1) for b in range(a + 1) for c in range(b + 1)
    ]
    place = {t: i for i, t in enumerate(triples)}
    edges = []
    for t in triples:
        used = [x for x in t if x]
        mine = []
        for k in range(1, modes + 1):
            power = used.count(k)
            if len(used) < DEGREE:
                up = tuple(sorted(used + [k], reverse=True))
                mine.append((place[up + (0,) * (DEGREE - len(up))], k - 1, power + 1))
            if power:
                left = list(used)
                left.remove(k)
                mine.append((place[tuple(left) + (0,) * (DEGREE - len(left))], k - 1, power))
        edges.append(mine)
    return edges


def rank_row(powers):
    modes, here = powers.shape
    above = jnp.zeros((1, here), jnp.int32)
    symbols = [jnp.zeros((1, here), jnp.int32)] * DEGREE
    for k in reversed(range(modes)):
        above += jnp.maximum(powers[k : k + 1], 0)
        symbols = [a + jnp.where(above > n, 1, 0) for n, a in enumerate(symbols)]
    a, b, c = symbols
    rank = a * (a + 1) * (a + 2) // 6 + b * (b + 1) // 2 + c
    return jnp.where(powers[0:1] < 0, math.comb(modes + DEGREE, DEGREE), rank).astype(jnp.float32)


def cut_kernel(n, columns, rows, offsets_ref, source_ref, *refs):
    per = SUB // columns
    index, parts = refs[:-n], refs[-n:]
    for d, out in enumerate(parts):
        at = pl.ds(pl.multiple_of(offsets_ref[d], columns), columns)
        for g in range(per):
            for q in range(rows):
                out[q, g * columns : (g + 1) * columns] = source_ref[q * per + g, at]
    if index:
        ranks = rank_row(index[0][...])
        for out in parts:
            out[rows] = jnp.zeros((SUB, LANES), jnp.float32)
            out[rows, 0:1, 0 : ranks.shape[1]] = ranks


def lane_next(u):
    lane = lax.broadcasted_iota(jnp.int32, u.shape, u.ndim - 1)
    return jnp.where(lane == LANES - 1, 0.0, pltpu.roll(u, LANES - 1, u.ndim - 1))


def lane_before(u):
    lane = lax.broadcasted_iota(jnp.int32, u.shape, u.ndim - 1)
    return jnp.where(lane == 0, 0.0, pltpu.roll(u, 1, u.ndim - 1))


def face_coefficients(coef_ref):
    east, right, left = [], [], []
    for k in range(coef_ref.shape[0]):
        c = coef_ref[k]
        east.append(0.5 * (c + pltpu.roll(c, SUB - 1, 0)))
        right.append(0.5 * (c + lane_next(c)))
        left.append(0.5 * (c + lane_before(c)))
    return east, right, left


def apply_operator(u_ref, coef_ref, edges, store, diff_ref):
    terms = len(edges)

    u = u_ref[0:terms]
    diff_ref[0, 0:terms] = pltpu.roll(u, SUB - 1, 1) - u
    diff_ref[1, 0:terms] = u - lane_next(u)
    diff_ref[2, 0:terms] = u - lane_before(u)
    east, right, left = face_coefficients(coef_ref)
    for s in range(terms):
        groups = {1: [(s, 0)]}
        for t, k, weight in edges[s]:
            groups.setdefault(weight, []).append((t, k + 1))
        across = along = None
        for weight, members in groups.items():
            e = a = None
            for t, k in members:
                de = east[k] * diff_ref[0, t]
                da = right[k] * diff_ref[1, t] + left[k] * diff_ref[2, t]
                e = de if e is None else e + de
                a = da if a is None else a + da
            if weight > 1:
                e, a = e * math.sqrt(weight), a * math.sqrt(weight)
            across = e if across is None else across + e
            along = a if along is None else along + a
        store(s, pltpu.roll(across, 1, 0) - across + along)


def pack_rows(ranks_ref, packed_refs, field_ref, columns, rows, first=0):
    per = SUB // columns
    sub = lax.broadcasted_iota(jnp.int32, (SUB, LANES), 0)
    for d, out in enumerate(packed_refs):

        def one(q, carry, d=d, out=out):
            row = field_ref[ranks_ref[(d * rows + q) * per]]
            for g in range(1, per):
                other = field_ref[ranks_ref[(d * rows + q) * per + g]]
                row = jnp.where(sub < g * columns, row, pltpu.roll(other, g * columns, 0))
            out[first + q] = row
            return carry

        lax.fori_loop(0, rows, one, 0, unroll=min(rows, UNROLL))


def scatter_row(ranks_ref, at, row, field_ref, columns):
    per = SUB // columns
    for g in range(per):
        part = row if g == 0 else pltpu.roll(row, SUB - g * columns, 0)
        field_ref[ranks_ref[at * per + g], 0:columns] = part[0:columns]


def take_column(flat_ref, j, rows):
    return flat_ref[pl.ds(j, rows, stride=SUB), :]


def enter_kernel(n, columns, rows, ranks_ref, coef_ref, *refs):
    parts, (field_ref, first_ref, last_ref) = refs[:n], refs[n:]
    slots = field_ref.shape[0]
    fields = coef_ref.shape[0]
    field_ref[...] = jnp.zeros_like(field_ref)
    for d, part in enumerate(parts):

        def one(q, carry, d=d, part=part):
            scatter_row(ranks_ref, d * rows + q, part[q], field_ref, columns)
            return carry

        lax.fori_loop(0, rows, one, 0, unroll=min(rows, UNROLL))
    flat = field_ref.reshape(slots * SUB, LANES)
    terms = first_ref.shape[0] - 2 * fields
    first_ref[0:terms] = take_column(flat, 0, terms)
    last_ref[0:terms] = take_column(flat, columns - 1, terms)
    flat = coef_ref.reshape(fields * SUB, LANES)
    for j in range(2):
        at = terms + j * fields
        first_ref[at : at + fields] = take_column(flat, j, fields)
        last_ref[at : at + fields] = take_column(flat, columns - 2 + j, fields)


def start_kernel(n, columns, rows, edges, ranks_ref, x_ref, before_ref, after_ref, own_ref, *refs):
    residual_refs, (coef_ref, u_ref, y_ref, diff_ref) = refs[:-4], refs[-4:]
    slots, fields, terms = x_ref.shape[0], own_ref.shape[0], len(edges)
    coef_ref[...] = own_ref[...]
    flat = coef_ref.reshape(fields * SUB, LANES)
    for j in range(2):
        at = terms + j * fields
        flat[pl.ds(SUB - 2 + j, fields, stride=SUB), :] = before_ref[at : at + fields]
        flat[pl.ds(columns + j, fields, stride=SUB), :] = after_ref[at : at + fields]
    u_ref[...] = x_ref[...]
    flat = u_ref.reshape(slots * SUB, LANES)
    flat[pl.ds(SUB - 1, terms, stride=SUB), :] = before_ref[0:terms]
    flat[pl.ds(columns, terms, stride=SUB), :] = after_ref[0:terms]
    y_ref[len(edges) :] = jnp.zeros((slots - len(edges), SUB, LANES), jnp.float32)

    def store(s, value):
        y_ref[s] = value

    apply_operator(u_ref, coef_ref, edges, store, diff_ref)
    residual(n, columns, rows, ranks_ref, y_ref, *residual_refs)


def residual(n, columns, rows, ranks_ref, y_ref, *refs):
    forcing, packed, (field_ref, first_ref, last_ref) = refs[:n], refs[n : 2 * n], refs[2 * n :]
    per = SUB // columns
    slots = field_ref.shape[0]
    sub = lax.broadcasted_iota(jnp.int32, (SUB, LANES), 0)
    field_ref[...] = jnp.zeros_like(field_ref)
    for d in range(n):

        def one(q, carry, d=d):
            at = [ranks_ref[(d * rows + q) * per + g] for g in range(per)]
            y = y_ref[at[0]]
            for g in range(1, per):
                y = jnp.where(sub < g * columns, y, pltpu.roll(y_ref[at[g]], g * columns, 0))
            v = forcing[d][q] - y
            packed[d][q] = v
            for g in range(per):
                own = v if g == 0 else pltpu.roll(v, SUB - g * columns, 0)
                field_ref[at[g], 0:columns] = own[0:columns]
            return carry

        lax.fori_loop(0, rows, one, 0, unroll=min(rows, UNROLL))
    flat = field_ref.reshape(slots * SUB, LANES)
    for j in range(2):
        first_ref[j] = take_column(flat, j, slots)
        last_ref[j] = take_column(flat, columns - 2 + j, slots)


def krylov_kernel(
    n, columns, edges, ranks_ref, place_ref, v_ref, before_ref, after_ref, coef_ref, inside_ref, *refs
):
    packed, (table_ref, v0_ref, v1_ref, v2_ref, diff_ref) = refs[:n], refs[n:]
    rows = packed[0].shape[0] // 2
    slots, terms = v_ref.shape[0], len(edges)
    v0_ref[...] = v_ref[...]
    flat = v0_ref.reshape(slots * SUB, LANES)
    for j in range(2):
        flat[pl.ds(SUB - 2 + j, slots, stride=SUB), :] = before_ref[j]
        flat[pl.ds(columns + j, slots, stride=SUB), :] = after_ref[j]
    inside = inside_ref[...] > 0.0

    def store_first(s, value):
        v1_ref[s] = jnp.where(inside, value, 0.0)

    def store_second(s, value):
        v2_ref[s] = value

    for source, target, store in ((v0_ref, v1_ref, store_first), (v1_ref, v2_ref, store_second)):
        target[terms:] = jnp.zeros((slots - terms, SUB, LANES), jnp.float32)
        apply_operator(source, coef_ref, edges, store, diff_ref)
    pack_rows(ranks_ref, packed, v1_ref, columns, rows)
    pack_rows(ranks_ref, packed, v2_ref, columns, rows, rows)
    dot_products(place_ref, columns, v0_ref, v1_ref, v2_ref, table_ref)


def own_sums(count, terms, columns, of_term):
    def one(s, totals):
        return tuple(t + x for t, x in zip(totals, of_term(s)))

    totals = lax.fori_loop(0, terms, one, (jnp.zeros((SUB, LANES), jnp.float32),) * count, unroll=16)
    own = lax.broadcasted_iota(jnp.int32, (SUB, LANES), 0) < columns
    totals = [jnp.where(own, t, 0.0) for t in totals]
    return [jnp.sum(jnp.sum(t, axis=0, keepdims=True), axis=1, keepdims=True) for t in totals]


def dot_products(place_ref, columns, v0_ref, v1_ref, v2_ref, table_ref):
    slots = v0_ref.shape[0]
    aa, ab = own_sums(2, slots, columns, lambda s: (v0_ref[s] * v0_ref[s], v0_ref[s] * v1_ref[s]))
    m = jnp.where(aa > 0.0, ab / jnp.where(aa > 0.0, aa, 1.0), 0.0)

    def products(s):
        a, b, c = v0_ref[s], v1_ref[s], v2_ref[s]
        w = b - m * a
        e = c - m * b
        return a * w, w * w, a * e, w * b, w * e

    entries = [aa, ab, m] + own_sums(5, slots, columns, products)
    lane = lax.broadcasted_iota(jnp.int32, table_ref.shape, 1)
    row = lax.broadcasted_iota(jnp.int32, table_ref.shape, 0)
    table = jnp.zeros(table_ref.shape, jnp.float32)
    for k, value in enumerate(entries):
        table = jnp.where(lane == k, value, table)
    table_ref[...] = jnp.where(row == place_ref[0], table, 0.0)


def step_lengths(table):
    lane = lax.broadcasted_iota(jnp.int32, table.shape, 1)
    aa, ab, m, aw, ww, ae, wb, we = (
        jnp.sum(jnp.where(lane == k, table, 0.0), axis=1, keepdims=True) for k in range(8)
    )

    def total(x):
        return jnp.sum(x, axis=0, keepdims=True)

    norm, curve = total(aa), total(ab)
    step = norm / curve
    g = 1.0 - step * m
    rr = total(g * g * aa - 2.0 * g * step * aw + step * step * ww)
    r_ar = total(g * g * ab - g * step * (ae + wb) + step * step * we)
    mixed = total(2.0 * g * ab - step * (wb + ae))
    beta = rr / norm
    return step, beta, rr / (r_ar + beta * mixed + beta * beta * curve)


def finish_kernel(n, columns, offsets_ref, x_ref, *refs):
    tables, v0, krylov = refs[:n], refs[n : 2 * n], refs[2 * n : 3 * n]
    approx_ref, residual_ref = refs[3 * n :]
    per = SUB // columns
    rows = v0[0].shape[0]
    step, beta, last = step_lengths(functools.reduce(jnp.add, [t[...] for t in tables]))
    whole = step + last * beta
    for d in range(n):
        at = pl.ds(pl.multiple_of(offsets_ref[d], columns), columns)

        def one(q, carry, d=d, at=at):
            a, b, c = v0[d][q], krylov[d][q], krylov[d][rows + q]
            for g in range(per):
                part = slice(g * columns, (g + 1) * columns)
                s = q * per + g
                ag, bg, cg = a[part], b[part], c[part]
                r1 = ag - step * bg
                approx_ref[s, at] = x_ref[s, at] + whole * ag + last * r1
                residual_ref[s, at] = r1 - last * ((1.0 + beta) * bg - step * cg)
            return carry

        lax.fori_loop(0, rows, one, 0, unroll=min(rows, UNROLL))


class Anywhere:
    def __init__(self, value):
        self.value = value


def call(kernel, scalars, arrays, outs, scratch=()):
    whole = pl.BlockSpec(memory_space=pltpu.VMEM)
    specs = [
        pl.BlockSpec(memory_space=pl.ANY) if isinstance(a, Anywhere) else whole for a in arrays
    ]
    arrays = [a.value if isinstance(a, Anywhere) else a for a in arrays]
    return pl.pallas_call(
        kernel,
        in_specs=[pl.BlockSpec(memory_space=pltpu.SMEM)] * len(scalars) + specs,
        out_specs=[whole] * len(outs),
        out_shape=[jax.ShapeDtypeStruct(s, jnp.float32) for s in outs],
        scratch_shapes=[pltpu.VMEM(s, jnp.float32) for s in scratch],
        compiler_params=PARAMS,
    )(*scalars, *arrays)


def butterfly(value, axis):
    count = lax.axis_size(axis)
    bit = 1
    while bit < count:
        value = value + lax.ppermute(value, axis, [(i, i ^ bit) for i in range(count)])
        bit *= 2
    return value


def per_device(forcing, start_guess, mean_field, mode_fields, multi_index, coupled_slot):
    spaces, n = lax.axis_size("space"), lax.axis_size("chaos")
    i, z = lax.axis_index("space"), lax.axis_index("chaos")
    here, width, lanes = forcing.shape
    modes = mode_fields.shape[0]
    columns = width // n
    rows = here * columns // SUB
    slots = n * here
    edges = term_list(modes)

    def chunk(space, chaos):
        return jnp.where(space % 2 == 0, chaos, n - 1 - chaos)

    def device_at(p):
        tile, c = divmod(p, n)
        return tile * n + (c if tile % 2 == 0 else n - 1 - c)

    line = [(device_at(p), device_at(p + 1)) for p in range(spaces * n - 1)]
    back_line = [(b, a) for a, b in line]
    both = ("space", "chaos")

    def outward(d):
        return [(j, (j + d) % n) for j in range(n)]

    def homeward(d):
        return [(j, (j - d) % n) for j in range(n)]

    offsets = [columns * chunk(i, (z + d) % n) for d in range(n)]

    def longer(count):
        return [(count + (d == n // 2), SUB, lanes) for d in range(n)]

    def sent(parts, way, after=None):
        out = [parts[0]]
        for d in range(1, n):
            value = parts[d]
            if after is not None and after[d] is not None:
                value = lax.optimization_barrier((value, after[d]))[0]
            out.append(lax.ppermute(value, "chaos", way(d)))
        return out

    field, part, fields = (slots, SUB, lanes), (rows, SUB, lanes), (modes + 1, SUB, lanes)
    diff = (3,) + field
    edge = (len(edges) + 2 * (modes + 1), lanes)
    offsets_array = jnp.stack(offsets).astype(jnp.int32)

    f_rows = max(rows, edge[0] // SUB + 1)
    f_shapes = [(f_rows, SUB, lanes)] * n
    cut = functools.partial(cut_kernel, n, columns, rows)
    x_parts = call(cut, [offsets_array], [start_guess, multi_index.T], longer(rows + 1))
    x_parts = sent(list(x_parts), outward)
    ranks = jnp.concatenate([p[rows, 0, :here] for p in x_parts]).astype(jnp.int32)
    f_parts = sent(list(call(cut, [offsets_array], [forcing], f_shapes)), outward)

    stacked = jnp.concatenate([mean_field[None], mode_fields], axis=0)
    own_coef = lax.dynamic_slice_in_dim(stacked, offsets[0], columns, axis=1)
    own_coef = jnp.pad(own_coef, ((0, 0), (0, SUB - columns), (0, 0)))
    sub = lax.broadcasted_iota(jnp.int32, (SUB, lanes), 0)
    position = i * n + chunk(i, z)
    outside = ((position == 0) & (sub >= SUB - 2)) | (
        (position == spaces * n - 1) & (sub >= columns) & (sub < columns + 2)
    )
    inside = jnp.where(outside, 0.0, 1.0)

    x, x_first, x_last = call(
        functools.partial(enter_kernel, n, columns, rows),
        [ranks],
        [own_coef] + x_parts,
        [field, edge, edge],
    )
    x_before = lax.ppermute(x_last, both, line)
    x_after = lax.ppermute(x_first, both, back_line)
    *v0_parts, v0, v0_first, v0_last, coef = call(
        functools.partial(start_kernel, n, columns, rows, edges),
        [ranks],
        [x, x_before, x_after, own_coef] + f_parts,
        [part] * n + [field, (2, slots, lanes), (2, slots, lanes), fields],
        [field, field, diff],
    )
    v0_before = lax.ppermute(v0_last, both, line)
    v0_after = lax.ppermute(v0_first, both, back_line)
    v0_home = sent(v0_parts, homeward)
    table_rows = -(-spaces * n // SUB) * SUB
    *krylov, table = call(
        functools.partial(krylov_kernel, n, columns, edges),
        [ranks, (i * n + z).astype(jnp.int32)[None]],
        [v0, v0_before, v0_after, coef, inside],
        [(2 * rows, SUB, lanes)] * n + [(SPARE_ROWS + table_rows, lanes)],
        [field, field, field, diff],
    )
    far = n // 2
    near_home = [v0_home[d] for d in range(1, n) if d != far]
    krylov, near_home = lax.optimization_barrier((krylov, near_home))
    krylov_home = sent(krylov, homeward)
    table, v0_home[far] = lax.optimization_barrier((table, v0_home[far]))
    table = butterfly(table, "space")[:table_rows]
    tables = sent([table] * n, homeward, [None, krylov_home[n - 1]] + [None] * (n - 2))
    return call(
        functools.partial(finish_kernel, n, columns),
        [offsets_array],
        [start_guess] + tables + v0_home + krylov_home,
        [forcing.shape] * 2,
    )


def solution(mesh):
    placed = (
        P("chaos", "space", None),
        P("chaos", "space", None),
        P("space", None),
        P(None, "space", None),
        P("chaos", None),
        P("chaos", None),
    )
    return jax.shard_map(
        lambda *a: tuple(per_device(*a)),
        mesh=mesh,
        in_specs=placed,
        out_specs=(P("chaos", "space", None), P("chaos", "space", None)),
        check_vma=False,
    )
```
